512 devices in a mesh: tm: 32 (over y, x, z_hi), zone: 16 (over z_lo, core).
Axes of the slice: x: 4, y: 4, z: 16 (z_hi: 2, z_lo: 8; z = z_hi * 8 + z_lo), core: 2. Of those that a mesh axis runs over, the one named last changes fastest.
Arguments:
- states: bfloat16 [128, 2048, 512], P('tm', 'zone'), may hold values from -6 to 6
- gain_attn: float32 [512], replicated, may hold values from 0.1 to 1.9
- w_qkv: bfloat16 [512, 1536], P('zone')
- w_out_attn: bfloat16 [512, 512], P('zone'), may hold values from -0.25 to 0.25
- pattern: int32 [32, 2], P('tm'), may hold values from 0 to 1, as said below
- gain_mix: float32 [512], replicated, may hold values from 0.1 to 1.9
- neighbours: int32 [16, 3], replicated, may hold values from 0 to 15, as said below
- degree: int32 [16], replicated, may hold values from 1 to 3
- mix: bfloat16 [16, 3, 128, 128], replicated, may hold values from -0.3125 to 0.3125
- gain_ffn: float32 [512], replicated, may hold values from 0.1 to 1.9
- w_in: bfloat16 [512, 2048], P('zone'), may hold values from -0.25 to 0.25
- w_out: bfloat16 [2048, 512], P('zone'), may hold values from -0.125 to 0.125
Outputs:
- evolved: bfloat16 [128, 2048, 512], P('tm', 'zone')
The draws below stay inside these ranges and needn't reach their ends.
Inputs may be any that keep to these rules, and one draw needn't show every extreme that they name: `pattern`: time blocks 1 to 2 each attend to time block 0. `neighbours`: each row names 3 different zone blocks.
All inputs are finite; a program needn't handle non-finite values.
Results may differ from the reference program's by a relative error of at most 0.008.
Values may be sent and summed in bfloat16 or wider, within the bound.
A program may use at most 64 MiB of HBM per device.

```python
import math
import jax
import jax.numpy as jnp
from jax import lax

D = 512
HEADS = 4
FF = 2048
ZB = 128
T_DEV = 4
REACH = 2
KMAX = 3
HD = 128
TBLOCKS = 32
ZBLOCKS = 16
TIME = 128
ZONES = 2048


def draw_w_qkv(key, part):
    first = jax.random.fold_in(key, 0)
    base = jax.random.normal(first, (D, 3 * D), jnp.float32) / math.sqrt(D)
    return base.astype(jnp.bfloat16)


def draw_pattern(key, part):
    bits = jax.random.randint(jax.random.fold_in(key, 37), (TBLOCKS, REACH), 0, 2, jnp.int32)
    block_ids = jnp.arange(TBLOCKS, dtype=jnp.int32)[:, None]
    back_ids = jnp.arange(REACH, dtype=jnp.int32)[None, :] + 1
    return jnp.where(block_ids == back_ids, 1, bits).astype(jnp.int32)


def draw_neighbours(key, part):
    row_keys = jax.random.split(jax.random.fold_in(key, 11), ZBLOCKS)
    rows = jax.vmap(lambda row_key: jax.random.permutation(row_key, ZBLOCKS)[:KMAX])(row_keys)
    return rows.astype(jnp.int32)


def draw_degree(key, part):
    first, second = jax.random.split(jax.random.fold_in(key, 23))
    counts = jax.random.randint(first, (ZBLOCKS,), 1, KMAX + 1, jnp.int32)
    chosen = jax.random.randint(second, (), 0, ZBLOCKS, jnp.int32)
    return jnp.where(jnp.arange(ZBLOCKS, dtype=jnp.int32) == chosen, KMAX, counts).astype(jnp.int32)


def block_scale(rng, dims, shards, low, high):
    level, own = 1.0, jax.random.fold_in(rng, 6)
    for position, parts in shards:
        draws = jnp.exp(jax.random.uniform(jax.random.fold_in(own, position), (parts,), jnp.float32, low / len(shards), high / len(shards)))
        level = level * jnp.repeat(draws, dims[position] // parts).reshape([-1 if axis == position else 1 for axis in range(len(dims))])
    return level


def noise(own_key, shape, width, most, cuts=(), kind=jnp.bfloat16):
    level = block_scale(own_key, shape, cuts, -0.22, 0.18) if cuts else 1.0
    drawn = jax.random.normal(own_key, shape, jnp.float32) * width * level
    return jnp.minimum(jnp.maximum(drawn, -most), most).astype(kind)


def setup_inputs(seed: int = 0) -> dict:
    key_of = jax.random.split(jax.random.key(seed), 13)
    states = noise(key_of[0], (TIME, ZONES, D), 1.0, 6.0, ((0, 32), (1, 16)))
    gain_attn = jnp.clip(1.0 + 0.18 * jax.random.normal(key_of[1], (D,), jnp.float32), 0.1, 1.9)
    w_qkv = draw_w_qkv(jax.random.fold_in(key_of[12], 71), 0)
    w_out_attn = noise(key_of[3], (D, D), D ** -0.5, 0.25, ((0, 16),))
    pattern = draw_pattern(jax.random.fold_in(key_of[12], 71), 0)
    gain_mix = jnp.clip(1.0 + 0.18 * jax.random.normal(key_of[5], (D,), jnp.float32), 0.1, 1.9)
    neighbours = draw_neighbours(jax.random.fold_in(key_of[12], 71), 0)
    degree = draw_degree(jax.random.fold_in(key_of[12], 71), 0)
    mix = noise(key_of[8], (ZBLOCKS, KMAX, ZB, ZB), (ZB * KMAX) ** -0.5, 0.3125)
    gain_ffn = jnp.clip(1.0 + 0.18 * jax.random.normal(key_of[9], (D,), jnp.float32), 0.1, 1.9)
    w_in = noise(key_of[10], (D, FF), D ** -0.5, 0.25, ((0, 16),))
    w_out = noise(key_of[11], (FF, D), FF ** -0.5, 0.125, ((0, 16),))
    return dict(states=states, gain_attn=gain_attn, w_qkv=w_qkv, w_out_attn=w_out_attn, pattern=pattern, gain_mix=gain_mix, neighbours=neighbours, degree=degree, mix=mix, gain_ffn=gain_ffn, w_in=w_in, w_out=w_out)


def rms_scale(values, gain):
    mean_sq = lax.optimization_barrier(jnp.mean(values * values, axis=-1, keepdims=True))
    return values * lax.rsqrt(mean_sq + 1e-06) * gain

def attend_block(x_block, gain_attn, w_qkv, w_out_attn, pattern):
    steps = x_block.shape[0]
    x_wide = x_block.astype(jnp.float32)
    normed = rms_scale(x_wide, gain_attn).astype(jnp.bfloat16)
    projected = jnp.dot(normed.reshape(-1, D), w_qkv, preferred_element_type=jnp.float32).astype(jnp.bfloat16)
    projected = projected.reshape(steps, ZB, 3, HEADS, HD)
    queries = projected[:, :, 0].astype(jnp.float32)
    keys = projected[:, :, 1].astype(jnp.float32)
    values = projected[:, :, 2].astype(jnp.float32)
    scores = jnp.einsum('tzhd,szhd->zhts', queries, keys) * HD ** (-0.5)
    tpos = jnp.arange(steps, dtype=jnp.int32)
    qblock = tpos // T_DEV
    offset = qblock[:, None] - qblock[None, :]
    pattern_ext = jnp.concatenate([jnp.ones((TBLOCKS, 1), jnp.int32), pattern.astype(jnp.int32), jnp.zeros((TBLOCKS, 1), jnp.int32)], axis=1)
    clipped = jnp.clip(offset, 0, REACH + 1)
    allowed = (tpos[None, :] <= tpos[:, None]) & (offset <= REACH) & (pattern_ext[qblock[:, None], clipped] == 1)
    masked = jnp.where(allowed, scores, -1e+30)
    top = lax.optimization_barrier(jnp.max(masked, axis=-1, keepdims=True))
    expw = jnp.where(allowed, jnp.exp(masked - top), 0.0)
    total = lax.optimization_barrier(jnp.sum(expw, axis=-1))
    probs = expw.astype(jnp.bfloat16).astype(jnp.float32)
    context = jnp.einsum('zhts,szhd->tzhd', probs, values) / jnp.transpose(total, (2, 0, 1))[..., None]
    context = context.astype(jnp.bfloat16).reshape(-1, D)
    return x_wide + jnp.dot(context, w_out_attn, preferred_element_type=jnp.float32).reshape(steps, ZB, D)

def reference(states, gain_attn, w_qkv, w_out_attn, pattern, gain_mix, neighbours, degree, mix, gain_ffn, w_in, w_out):

    def section_one(block):
        x_block = lax.dynamic_slice_in_dim(states, (block * ZB).astype(jnp.int32), ZB, 1)
        return attend_block(x_block, gain_attn, w_qkv, w_out_attn, pattern)
    blocks = lax.map(section_one, jnp.arange(ZBLOCKS, dtype=jnp.int32))
    after_attn = jnp.transpose(blocks, (1, 0, 2, 3)).reshape(TIME, ZONES, D)
    slot_live = jnp.arange(KMAX, dtype=jnp.int32)[None, :] < degree[:, None]
    live_mix = jnp.where(slot_live[:, :, None, None], mix.astype(jnp.float32), 0.0)

    def section_two(row):
        mixin = rms_scale(row, gain_mix).astype(jnp.bfloat16).reshape(ZBLOCKS, ZB, D)
        nearby = mixin[neighbours].astype(jnp.float32)
        spatial = jnp.einsum('bkzy,bkyd->bzd', live_mix, nearby).astype(jnp.bfloat16).reshape(ZONES, D)
        after_mix = row + spatial.astype(jnp.float32)
        ffn_in = rms_scale(after_mix, gain_ffn).astype(jnp.bfloat16)
        hidden = jax.nn.gelu(jnp.dot(ffn_in, w_in, preferred_element_type=jnp.float32), approximate=True).astype(jnp.bfloat16)
        return (after_mix + jnp.dot(hidden, w_out, preferred_element_type=jnp.float32)).astype(jnp.bfloat16)
    return lax.map(section_two, after_attn)
```

```python
import functools

import jax
import jax.numpy as jnp
from jax import lax
from jax.experimental import pallas as pl
from jax.experimental.pallas import tpu as pltpu
from jax.sharding import PartitionSpec as P

MESH = pl.DeviceIdType.MESH
HEADS = 4
HD = 128
NG = 4
ZC = 32
F32, BF16 = jnp.float32, jnp.bfloat16

SLOTS = [(d, f, 0) for d in (3, -3, 2, -2, 1, -1, 0) for f in (0, 1) if (d, f) != (0, 0)]
SLOTS += [(d, f, 1) for d in (4, -4) for f in (0, 1)]
RING = (-3, 3, 4, -2, 2, -1, 1)
XY = [(dx, dy) for dx in range(4) for dy in range(4) if dx or dy]


def rms(values, gain):
    mean_sq = jnp.mean(values * values, axis=-1, keepdims=True)
    return values * lax.rsqrt(mean_sq + 1e-06) * gain


def dot(a, b):
    return jnp.dot(a, b, preferred_element_type=F32)


def kernel(
    states, w_qkv, w_attn, w_in, w_out, mix, pat, g_attn, g_mix, g_ffn, neighbours, degree,
    out,
    st, wq, wa, wi, wo, mx, pats, nrm, kv, qs, ctx, aa, after, mixin, xm, stage, spat, nf, acc,
    loc_sem, ag1_s, ag1_r, ag2_s, ag2_r, ag3_s, ag3_r, e1_s, e1_r, ep_s, ep_r, e2_s, e2_r,
    fw_s, fw_r, rt_s, rt_r,
):
    tm, zone = lax.axis_index("tm"), lax.axis_index("zone")
    h, col = lax.rem(tm, 2), tm // 2
    x, y = lax.rem(col, 4), col // 4
    zl, c = zone // 2, lax.rem(zone, 2)
    z = h * 8 + zl
    p = col

    def at_z(d, flip):
        zz = lax.rem(z + d + 16, 16)
        return (col * 2 + zz // 8, lax.rem(zz, 8) * 2 + lax.rem(c + flip, 2))

    def at_xy(dx, dy):
        xx, yy = lax.rem(x + dx, 4), lax.rem(y + dy, 4)
        return ((yy * 4 + xx) * 2 + h, zone)

    following = (lax.rem(col + 1, 16) * 2 + h, zone)
    partner = at_z(8, 0)
    other = at_z(0, 1)

    def remote(src, dst, ssem, rsem, dev):
        return pltpu.make_async_remote_copy(
            src, dst, ssem, rsem, device_id=dev, device_id_type=MESH
        )

    locals_ = [
        pltpu.make_async_copy(states, st.at[2 + h], loc_sem.at[0]),
        pltpu.make_async_copy(mix, mx, loc_sem.at[1]),
    ]
    r8, c8 = p // 8, pl.multiple_of(lax.rem(p, 8) * 128, 128)
    p8 = lax.rem(p, 8)
    r4, c4 = p8 // 4, pl.multiple_of(lax.rem(p8, 4) * 128, 128)
    i8 = pl.multiple_of(lax.rem(p, 8) * 256, 256)
    g2, h2 = p // 2, pl.multiple_of(lax.rem(p, 2) * 256, 256)
    first = p < 8

    src_kv = w_qkv.at[pl.ds(pl.multiple_of(r8 * 16, 16), 16), pl.ds(512 + c8, 128)]
    src_q = w_qkv.at[pl.ds(pl.multiple_of(r4 * 16, 16), 16), pl.ds(c4, 128)]
    src_a = w_attn.at[pl.ds(pl.multiple_of(r4 * 16, 16), 16), pl.ds(c4, 128)]
    src_i = w_in.at[pl.ds(pl.multiple_of(r8 * 16, 16), 16), pl.ds(i8, 256)]
    src_o = w_out.at[pl.ds(pl.multiple_of(g2 * 16, 16), 16), pl.ds(h2, 256)]

    def own_kv(zz):
        return wq.at[zz, c, r8, :, pl.ds(512 + c8, 128)]

    def own_q(zz):
        return wq.at[zz, c, r4, :, pl.ds(c4, 128)]

    def own_a(zz):
        return wa.at[zz, c, r4, :, pl.ds(c4, 128)]

    def own_i(zz):
        return wi.at[zz, c, r8, :, pl.ds(i8, 256)]

    def own_o(zz):
        return wo.at[zz, c, g2, :, pl.ds(h2, 256)]

    pieces = ((src_kv, own_kv), (src_i, own_i), (src_o, own_o))
    every = pl.ds(0, 8)

    for cp in locals_:
        cp.start()
    for n, (src, own) in enumerate(pieces):
        pltpu.make_async_copy(src, own(zl), loc_sem.at[2 + n]).start()

    @pl.when(first)
    def _():
        pltpu.make_async_copy(src_q, own_q(zl), loc_sem.at[5]).start()

    @pl.when(jnp.logical_not(first))
    def _():
        pltpu.make_async_copy(src_a, own_a(zl), loc_sem.at[5]).start()

    barrier = pltpu.get_barrier_semaphore()
    for d in range(16):
        for f in (0, 1):
            if (d, f) != (0, 0):
                pl.semaphore_signal(barrier, inc=1, device_id=at_z(d, f), device_id_type=MESH)
    for dx, dy in XY:
        pl.semaphore_signal(barrier, inc=1, device_id=at_xy(dx, dy), device_id_type=MESH)
    pl.semaphore_wait(barrier, 46)

    def chunk(ref, g):
        return ref.at[:, pl.ds(pl.multiple_of(g * ZC, ZC), ZC), :]

    def swap(g):
        return remote(chunk(states, g), chunk(st.at[2 + h], g), e1_s.at[g], e1_r.at[g], partner)

    def swapped(g):
        return remote(chunk(states, g), chunk(st.at[3 - h], g), e1_s.at[g], e1_r.at[g], partner)

    def onward(g):
        return remote(
            chunk(states, g), chunk(st.at[h], g), e2_s.at[0, g], e2_r.at[0, g], following
        )

    def relay(g):
        return remote(
            chunk(st.at[3 - h], g), chunk(st.at[1 - h], g), e2_s.at[1, g], e2_r.at[1, g], following
        )

    def ag1(n, src, own, k):
        return remote(src, own(zl), ag1_s.at[n, k], ag1_r.at[n, k], at_z(RING[k], 0))

    send_pat = remote(pat, pats.at[h], ep_s, ep_r, partner)
    send_pat.start()
    swap(0).start()
    for k in range(7):
        ag1(0, src_kv, own_kv, k).start()

    @pl.when(first)
    def _():
        for k in range(7):
            ag1(3, src_q, own_q, k).start()

    @pl.when(jnp.logical_not(first))
    def _():
        for k in range(7):
            ag1(3, src_a, own_a, k).start()

    for g in range(NG):
        if g:
            swap(g).start()
        onward(g).start()
    for k in range(7):
        ag1(1, src_i, own_i, k).start()
        ag1(2, src_o, own_o, k).start()
    pats[pl.ds(h, 1)] = pat[...].reshape(1, 8, 128)

    def ag2(n, own, k):
        return remote(own(every), own(every), ag2_s.at[n, k], ag2_r.at[n, k], at_xy(*XY[k]))

    for n in (0, 3):
        src, own = pieces[0] if n == 0 else (src_q, own_q)
        pltpu.make_async_copy(src, own(zl), loc_sem.at[2 if n == 0 else 5]).wait()
        for k in range(7):
            ag1(n, src, own, k).wait_recv()
    for k in range(15):
        ag2(0, own_kv, k).start()

    @pl.when(first)
    def _():
        for k in range(15):
            ag2(3, own_q, k).start()

    @pl.when(jnp.logical_not(first))
    def _():
        for k in range(15):
            ag2(3, own_a, k).start()

    for k in range(15):
        ag2(0, own_kv, k).wait_recv()
        ag2(3, own_q, k).wait_recv()

    def ag3(n, w):
        return remote(w.at[:, c], w.at[:, c], ag3_s.at[n], ag3_r.at[n], other)

    ag3(0, wq).start()
    ag3(1, wa).start()
    for n in (1, 2):
        src, own = pieces[n]
        pltpu.make_async_copy(src, own(zl), loc_sem.at[2 + n]).wait()
        for k in range(7):
            ag1(n, src, own, k).wait_recv()
    locals_[0].wait()
    send_pat.wait_recv()
    ag3(0, wq).wait_recv()
    ag3(1, wa).wait_recv()
    wq2, wa2 = wq.reshape(512, 1536), wa.reshape(512, 512)

    rows = lax.broadcasted_iota(jnp.int32, (128, 128), 0)
    cols = lax.broadcasted_iota(jnp.int32, (128, 128), 1)
    same = lax.rem(rows, ZC) == lax.rem(cols, ZC)
    causal = same & (cols // ZC <= rows // ZC)

    def fw(slot, g):
        d, f, half = SLOTS[slot]
        zz = lax.rem(z + d + 16, 16)
        m = lax.rem(zz, 8) * 2 + lax.rem(c + f, 2)
        low = g * ZC + (ZC // 2 if d == -4 else 0)
        span = pl.ds(pl.multiple_of(low, 16), ZC // 2 if half else ZC)
        return remote(
            mixin.at[zz // 8, m // 4, lax.rem(m, 4), span],
            xm.at[zone, span],
            fw_s.at[slot],
            fw_r.at[slot],
            at_z(d, f),
        )

    def step(g, carry):
        z0 = pl.multiple_of(g * ZC, ZC)
        swapped(g).wait_recv()
        relay(g).start()
        onward(g).wait_recv()
        relay(g).wait_recv()
        for b in range(4):
            block = st[b, :, pl.ds(z0, ZC), :].reshape(128, 512).astype(F32)
            nrm[b * 128 : (b + 1) * 128, :] = rms(block, g_attn[...]).astype(BF16)
        for j in range(2):
            kv[:, j * 512 : (j + 1) * 512] = dot(
                nrm[...], wq2[:, (j + 1) * 512 : (j + 2) * 512]
            ).astype(BF16)
        qs[...] = dot(nrm[256:512, :], wq2[:, 0:512]).astype(BF16)
        for t in range(2):
            gone = (col * 2 + t) >= 1
            ok1 = jnp.where(gone, pats[t, 0:1, :], 0.0)
            ok2 = jnp.where((col * 2 + t) >= 2, pats[t, 4:5, :], 0.0)
            allowed = jnp.concatenate(
                [same & (ok2 > 0.5), same & (ok1 > 0.5), causal], axis=1
            )
            for hd in range(HEADS):
                q = qs[t * 128 : (t + 1) * 128, hd * HD : (hd + 1) * HD]
                k = kv[t * 128 : t * 128 + 384, hd * HD : (hd + 1) * HD]
                v = kv[t * 128 : t * 128 + 384, 512 + hd * HD : 512 + (hd + 1) * HD]
                s = lax.dot_general(q, k, (((1,), (1,)), ((), ())), preferred_element_type=F32)
                s = jnp.where(allowed, s * HD**-0.5, -1e30)
                e = jnp.exp(s - jnp.max(s, axis=-1, keepdims=True))
                total = jnp.sum(e, axis=-1, keepdims=True)
                got = dot(e.astype(BF16), v) / total
                ctx[t * 128 : (t + 1) * 128, hd * HD : (hd + 1) * HD] = got.astype(BF16)
        for t in range(2):
            block = st[2 + t, :, pl.ds(z0, ZC), :].reshape(128, 512).astype(F32)
            wide = block + dot(ctx[t * 128 : (t + 1) * 128, :], wa2[...])
            aa[t] = wide
            mi = rms(wide, g_mix[...]).astype(BF16)
            for j in range(4):
                mixin[t, :, j, pl.ds(z0, ZC), :] = mi[:, j * 128 : (j + 1) * 128].reshape(
                    4, ZC, 128
                )
        for slot in range(len(SLOTS)):
            fw(slot, g).start()
        after[:, pl.ds(z0, ZC), :] = aa[h].reshape(4, ZC, 512)
        xm[zone, pl.ds(z0, ZC), :] = mixin[h, zone // 4, lax.rem(zone, 4), pl.ds(z0, ZC), :]
        return carry

    lax.fori_loop(0, NG, step, 0)

    for k in range(15):
        ag2(1, own_i, k).start()
        ag2(2, own_o, k).start()

    locals_[1].wait()
    for slot, (d, f, half) in enumerate(SLOTS):
        span = pl.ds(0, 64 if half else 128)
        remote(
            mixin.at[0, 0, 0, span], xm.at[zone, span], fw_s.at[slot], fw_r.at[slot], other
        ).wait()

    def mixed(b):
        total = jnp.zeros((128, 128), F32)
        for k in range(3):
            weight = mx[b, k]
            live = jnp.where(k < degree[b], weight, jnp.zeros_like(weight))
            total += dot(live, xm[neighbours[b, k]])
        return total.astype(BF16)

    def back(o):
        b = lax.rem(zone + o, 16)
        return remote(stage.at[b], spat.at[zone], rt_s.at[o], rt_r.at[o], (tm, b))

    def send_back(o, carry):
        b = lax.rem(zone + o, 16)
        stage[b] = mixed(b)
        back(o).start()
        return carry

    lax.fori_loop(1, 16, send_back, 0)
    spat[zone] = mixed(zone)

    for k in range(15):
        ag2(1, own_i, k).wait_recv()
        ag2(2, own_o, k).wait_recv()
    ag3(2, wi).start()
    ag3(3, wo).start()

    send_pat.wait_send()
    for g in range(NG):
        swap(g).wait_send()
        onward(g).wait_send()
        relay(g).wait_send()
    for k in range(7):
        ag1(0, src_kv, own_kv, k).wait_send()
        ag1(1, src_i, own_i, k).wait_send()
        ag1(2, src_o, own_o, k).wait_send()
        ag1(3, src_q, own_q, k).wait_send()
    for k in range(15):
        ag2(0, own_kv, k).wait_send()
        ag2(1, own_i, k).wait_send()
        ag2(2, own_o, k).wait_send()
        ag2(3, own_q, k).wait_send()
    ag3(0, wq).wait_send()
    ag3(1, wa).wait_send()
    ag3(2, wi).wait()
    ag3(3, wo).wait()

    wi2, wo2 = wi.reshape(512, 2048), wo.reshape(2048, 512)
    for o in range(1, 16):
        back(o).wait()
    for half in range(2):
        for i in range(2):
            t = half * 2 + i
            wide = after[t] + jnp.concatenate(
                [spat[t * 4 + j].astype(F32) for j in range(4)], axis=1
            )
            acc[i * 128 : (i + 1) * 128, :] = wide
            nf[i * 128 : (i + 1) * 128, :] = rms(wide, g_ffn[...]).astype(BF16)
        for j in range(4):
            hidden = jax.nn.gelu(
                dot(nf[...], wi2[:, j * 512 : (j + 1) * 512]), approximate=True
            ).astype(BF16)
            acc[...] += dot(hidden, wo2[j * 512 : (j + 1) * 512, :])
        out[half * 2 : half * 2 + 2] = acc[...].astype(BF16).reshape(2, 128, 512)


def on_device(
    states, gain_attn, w_qkv, w_out_attn, pattern, gain_mix, neighbours, degree, mix, gain_ffn,
    w_in, w_out,
):
    pat = jnp.broadcast_to(
        jnp.repeat(pattern.reshape(2, 1).astype(F32), 4, axis=0), (8, 128)
    )
    hbm = pl.BlockSpec(memory_space=pl.ANY)
    vmem = pl.BlockSpec(memory_space=pltpu.VMEM)
    smem = pl.BlockSpec(memory_space=pltpu.SMEM)
    dma = pltpu.SemaphoreType.DMA
    return pl.pallas_call(
        kernel,
        out_shape=jax.ShapeDtypeStruct(states.shape, BF16),
        in_specs=[hbm] * 6 + [vmem] * 4 + [smem] * 2,
        out_specs=vmem,
        scratch_shapes=[
            pltpu.VMEM((4, 4, 128, 512), BF16),
            pltpu.VMEM((8, 2, 2, 16, 1536), BF16),
            pltpu.VMEM((8, 2, 2, 16, 512), BF16),
            pltpu.VMEM((8, 2, 2, 16, 2048), BF16),
            pltpu.VMEM((8, 2, 8, 16, 512), BF16),
            pltpu.VMEM((16, 3, 128, 128), BF16),
            pltpu.VMEM((2, 8, 128), F32),
            pltpu.VMEM((512, 512), BF16),
            pltpu.VMEM((512, 1024), BF16),
            pltpu.VMEM((256, 512), BF16),
            pltpu.VMEM((256, 512), BF16),
            pltpu.VMEM((2, 128, 512), F32),
            pltpu.VMEM((4, 128, 512), F32),
            pltpu.VMEM((2, 4, 4, 128, 128), BF16),
            pltpu.VMEM((16, 128, 128), BF16),
            pltpu.VMEM((16, 128, 128), BF16),
            pltpu.VMEM((16, 128, 128), BF16),
            pltpu.VMEM((256, 512), BF16),
            pltpu.VMEM((256, 512), F32),
            dma((6,)),
            dma((4, 7)), dma((4, 7)),
            dma((4, 15)), dma((4, 15)),
            dma((4,)), dma((4,)),
            dma((NG,)), dma((NG,)),
            dma, dma,
            dma((2, NG)), dma((2, NG)),
            dma((len(SLOTS),)), dma((len(SLOTS),)),
            dma((16,)), dma((16,)),
        ],
        compiler_params=pltpu.CompilerParams(
            collective_id=0, has_side_effects=True, vmem_limit_bytes=48 << 20
        ),
        cost_estimate=pl.CostEstimate(
            flops=5 * 10**9, bytes_accessed=8 * 10**6, transcendentals=2 * 10**6
        ),
        name="layer",
    )(
        states, w_qkv, w_out_attn, w_in, w_out, mix, pat,
        gain_attn.reshape(1, -1), gain_mix.reshape(1, -1), gain_ffn.reshape(1, -1),
        neighbours, degree,
    )


def solution(mesh):
    return jax.shard_map(
        on_device,
        mesh=mesh,
        in_specs=(
            P("tm", "zone", None),
            P(),
            P("zone", None),
            P("zone", None),
            P("tm", None),
            P(),
            P(),
            P(),
            P(),
            P(),
            P("zone", None),
            P("zone", None),
        ),
        out_specs=P("tm", "zone", None),
        check_vma=False,
    )
```

```python
import functools

import jax
import jax.numpy as jnp
from jax import lax
from jax.experimental import pallas as pl
from jax.experimental.pallas import tpu as pltpu
from jax.sharding import PartitionSpec as P

MESH = pl.DeviceIdType.MESH
HEADS = 4
HD = 128
NG = 8
ZC = 16
R = 4 * ZC
F32, BF16 = jnp.float32, jnp.bfloat16

SLOTS = [(d, f) for d in (4, 3, -3, 2, -2, 1, -1, 0) for f in (0, 1) if (d, f) != (0, 0)]
RING = (-3, 3, 4, -2, 2, -1, 1)
XY = [(dx, dy) for dx in range(4) for dy in range(4) if dx or dy]


def rms(values, gain):
    mean_sq = jnp.mean(values * values, axis=-1, keepdims=True)
    return values * lax.rsqrt(mean_sq + 1e-06) * gain


def dot(a, b):
    return jnp.dot(a, b, preferred_element_type=F32)


def kernel(
    states, w_qkv, w_attn, w_in, w_out, mix, gains_a, gains_m, gains_f, pat_in, near_in, degree_in,
    out,
    pat, g_attn, g_mix, g_ffn, pattern, neighbours, degree, st, wq, wa, wi, wo, mx, pats, nrm, kv, qs, ctx, aa, after, mixin, xm, stage, spat, nf, acc,
    loc_sem, ag1_s, ag1_r, ag2_s, ag2_r, ag3_s, ag3_r, e1_s, e1_r, ep_s, ep_r, e2_s, e2_r,
    fw_s, fw_r, rt_s, rt_r,
):
    tm, zone = lax.axis_index("tm"), lax.axis_index("zone")
    h, col = lax.rem(tm, 2), tm // 2
    x, y = lax.rem(col, 4), col // 4
    zl, c = zone // 2, lax.rem(zone, 2)
    z = h * 8 + zl
    p = col

    def at_z(d, flip):
        zz = lax.rem(z + d + 16, 16)
        return (col * 2 + zz // 8, lax.rem(zz, 8) * 2 + lax.rem(c + flip, 2))

    def at_xy(dx, dy):
        xx, yy = lax.rem(x + dx, 4), lax.rem(y + dy, 4)
        return ((yy * 4 + xx) * 2 + h, zone)

    following = (lax.rem(col + 1, 16) * 2 + h, zone)
    partner = at_z(8, 0)
    other = at_z(0, 1)

    def remote(src, dst, ssem, rsem, dev):
        return pltpu.make_async_remote_copy(
            src, dst, ssem, rsem, device_id=dev, device_id_type=MESH
        )

    locals_ = [
        pltpu.make_async_copy(states, st.at[2 + h], loc_sem.at[0]),
        pltpu.make_async_copy(mix, mx, loc_sem.at[1]),
        pltpu.make_async_copy(pat_in, pattern, loc_sem.at[6]),
        pltpu.make_async_copy(gains_a, g_attn, loc_sem.at[7]),
        pltpu.make_async_copy(gains_m, g_mix, loc_sem.at[8]),
        pltpu.make_async_copy(gains_f, g_ffn, loc_sem.at[9]),
        pltpu.make_async_copy(near_in, neighbours, loc_sem.at[10]),
        pltpu.make_async_copy(degree_in, degree, loc_sem.at[11]),
    ]
    r8, c8 = p // 8, pl.multiple_of(lax.rem(p, 8) * 128, 128)
    p8 = lax.rem(p, 8)
    r4, c4 = p8 // 4, pl.multiple_of(lax.rem(p8, 4) * 128, 128)
    i8 = pl.multiple_of(lax.rem(p, 8) * 256, 256)
    g2, h2 = p // 2, pl.multiple_of(lax.rem(p, 2) * 256, 256)
    first = p < 8

    src_kv = w_qkv.at[pl.ds(pl.multiple_of(r8 * 16, 16), 16), pl.ds(512 + c8, 128)]
    src_q = w_qkv.at[pl.ds(pl.multiple_of(r4 * 16, 16), 16), pl.ds(c4, 128)]
    src_a = w_attn.at[pl.ds(pl.multiple_of(r4 * 16, 16), 16), pl.ds(c4, 128)]
    src_i = w_in.at[pl.ds(pl.multiple_of(r8 * 16, 16), 16), pl.ds(i8, 256)]
    src_o = w_out.at[pl.ds(pl.multiple_of(g2 * 16, 16), 16), pl.ds(h2, 256)]

    def own_kv(zz):
        return wq.at[zz, c, r8, :, pl.ds(512 + c8, 128)]

    def own_q(zz):
        return wq.at[zz, c, r4, :, pl.ds(c4, 128)]

    def own_a(zz):
        return wa.at[zz, c, r4, :, pl.ds(c4, 128)]

    def own_i(zz):
        return wi.at[zz, c, r8, :, pl.ds(i8, 256)]

    def own_o(zz):
        return wo.at[zz, c, g2, :, pl.ds(h2, 256)]

    pieces = ((src_kv, own_kv), (src_i, own_i), (src_o, own_o))
    every = pl.ds(0, 8)

    for cp in locals_:
        cp.start()
    for n, (src, own) in enumerate(pieces):
        pltpu.make_async_copy(src, own(zl), loc_sem.at[2 + n]).start()

    @pl.when(first)
    def _():
        pltpu.make_async_copy(src_q, own_q(zl), loc_sem.at[5]).start()

    @pl.when(jnp.logical_not(first))
    def _():
        pltpu.make_async_copy(src_a, own_a(zl), loc_sem.at[5]).start()

    barrier = pltpu.get_barrier_semaphore()
    for d in range(16):
        for f in (0, 1):
            if (d, f) != (0, 0):
                pl.semaphore_signal(barrier, inc=1, device_id=at_z(d, f), device_id_type=MESH)
    for dx, dy in XY:
        pl.semaphore_signal(barrier, inc=1, device_id=at_xy(dx, dy), device_id_type=MESH)
    locals_[2].wait()
    upper = lax.broadcasted_iota(jnp.int32, (8, 256), 0) < 4
    pat[...] = jnp.where(upper, pattern[0, 0], pattern[0, 1]).astype(F32)
    pats[pl.ds(h, 1)] = pat[...].reshape(1, 8, 256)
    pl.semaphore_wait(barrier, 46)

    def chunk(ref, g):
        return ref.at[:, pl.ds(pl.multiple_of(g * ZC, ZC), ZC), :]

    def swap(g):
        return remote(chunk(states, g), chunk(st.at[2 + h], g), e1_s.at[g], e1_r.at[g], partner)

    def swapped(g):
        return remote(chunk(states, g), chunk(st.at[3 - h], g), e1_s.at[g], e1_r.at[g], partner)

    def onward(g):
        return remote(
            chunk(states, g), chunk(st.at[h], g), e2_s.at[0, g], e2_r.at[0, g], following
        )

    def relay(g):
        return remote(
            chunk(st.at[3 - h], g), chunk(st.at[1 - h], g), e2_s.at[1, g], e2_r.at[1, g], following
        )

    def ag1(n, src, own, k):
        return remote(src, own(zl), ag1_s.at[n, k], ag1_r.at[n, k], at_z(RING[k], 0))

    send_pat = remote(pat, pats.at[h], ep_s, ep_r, partner)
    for k in range(7):
        ag1(0, src_kv, own_kv, k).start()

    @pl.when(first)
    def _():
        for k in range(7):
            ag1(3, src_q, own_q, k).start()

    @pl.when(jnp.logical_not(first))
    def _():
        for k in range(7):
            ag1(3, src_a, own_a, k).start()

    send_pat.start()
    for g in range(NG):
        swap(g).start()
        if g < 2:
            onward(g).start()

    def ag2(n, own, k):
        return remote(own(every), own(every), ag2_s.at[n, k], ag2_r.at[n, k], at_xy(*XY[k]))

    for n in (0, 3):
        src, own = pieces[0] if n == 0 else (src_q, own_q)
        pltpu.make_async_copy(src, own(zl), loc_sem.at[2 if n == 0 else 5]).wait()
        for k in range(7):
            ag1(n, src, own, k).wait_recv()
    for k in range(15):
        ag2(0, own_kv, k).start()

    @pl.when(first)
    def _():
        for k in range(15):
            ag2(3, own_q, k).start()

    @pl.when(jnp.logical_not(first))
    def _():
        for k in range(15):
            ag2(3, own_a, k).start()

    for g in range(2, NG):
        onward(g).start()
    for k in range(7):
        ag1(1, src_i, own_i, k).start()
        ag1(2, src_o, own_o, k).start()
    for k in range(15):
        ag2(0, own_kv, k).wait_recv()
        ag2(3, own_q, k).wait_recv()

    def ag3(n, w):
        return remote(w.at[:, c], w.at[:, c], ag3_s.at[n], ag3_r.at[n], other)

    ag3(0, wq).start()
    ag3(1, wa).start()
    locals_[0].wait()
    for n in (3, 4, 5, 6, 7):
        locals_[n].wait()
    send_pat.wait_recv()
    ag3(0, wq).wait_recv()
    ag3(1, wa).wait_recv()
    wq2, wa2 = wq.reshape(512, 1536), wa.reshape(512, 512)

    rows = lax.broadcasted_iota(jnp.int32, (R, 3 * R), 0)
    cols = lax.broadcasted_iota(jnp.int32, (R, 3 * R), 1)
    same = lax.rem(rows, ZC) == lax.rem(cols, ZC)
    segment = cols // R
    causal = same & (segment == 2) & (lax.rem(cols, R) // ZC <= rows // ZC)
    back1, back2 = same & (segment == 1), same & (segment == 0)

    def fw(slot, g):
        d, f = SLOTS[slot]
        if d == 4:
            d = 4 - 8 * lax.rem(g, 2)
        zz = lax.rem(z + d + 16, 16)
        m = lax.rem(zz, 8) * 2 + lax.rem(c + f, 2)
        span = pl.ds(pl.multiple_of(g * ZC, ZC), ZC)
        return remote(
            mixin.at[zz // 8, m // 4, lax.rem(m, 4), span],
            xm.at[zone, span],
            fw_s.at[slot],
            fw_r.at[slot],
            at_z(d, f),
        )

    swapped(0).wait_recv()
    relay(0).start()

    def step(g, carry):
        z0 = pl.multiple_of(g * ZC, ZC)

        @pl.when(g + 1 < NG)
        def _():
            swapped(g + 1).wait_recv()
            relay(g + 1).start()

        onward(g).wait_recv()
        relay(g).wait_recv()
        for b in range(4):
            block = st[b, :, pl.ds(z0, ZC), :].reshape(R, 512).astype(F32)
            nrm[b * R : (b + 1) * R, :] = rms(block, g_attn[...]).astype(BF16)
        for j in range(2):
            kv[:, j * 512 : (j + 1) * 512] = dot(
                nrm[...], wq2[:, (j + 1) * 512 : (j + 2) * 512]
            ).astype(BF16)
        qs[...] = dot(nrm[2 * R :, :], wq2[:, 0:512]).astype(BF16)
        pairs = [(t, hd) for t in range(2) for hd in range(HEADS)]
        scores = []
        for t, hd in pairs:
            q = qs[t * R : (t + 1) * R, hd * HD : (hd + 1) * HD]
            k = kv[t * R : (t + 3) * R, hd * HD : (hd + 1) * HD]
            scores.append(
                lax.dot_general(q, k, (((1,), (1,)), ((), ())), preferred_element_type=F32)
            )
        allowed = []
        for t in range(2):
            ok1 = jnp.where((col * 2 + t) >= 1, pats[t, 0:1, 0 : 3 * R], 0.0) > 0.5
            ok2 = jnp.where((col * 2 + t) >= 2, pats[t, 4:5, 0 : 3 * R], 0.0) > 0.5
            allowed.append(causal | (back1 & ok1) | (back2 & ok2))
        scores = [
            jnp.where(allowed[t], s * HD**-0.5, -1e30) for (t, _), s in zip(pairs, scores)
        ]
        tops = [jnp.max(s, axis=-1, keepdims=True) for s in scores]
        weights = [jnp.exp(s - top) for s, top in zip(scores, tops)]
        got = [
            dot(e.astype(BF16), kv[t * R : (t + 3) * R, 512 + hd * HD : 512 + (hd + 1) * HD])
            for (t, hd), e in zip(pairs, weights)
        ]
        totals = [jnp.sum(e, axis=-1, keepdims=True) for e in weights]
        for (t, hd), part, total in zip(pairs, got, totals):
            ctx[t * R : (t + 1) * R, hd * HD : (hd + 1) * HD] = (part / total).astype(BF16)
        both = dot(ctx[...], wa2[...])
        for t in range(2):
            block = st[2 + t, :, pl.ds(z0, ZC), :].reshape(R, 512).astype(F32)
            wide = block + both[t * R : (t + 1) * R, :]
            aa[t] = wide
            mi = rms(wide, g_mix[...]).astype(BF16)
            for j in range(4):
                mixin[t, :, j, pl.ds(z0, ZC), :] = mi[:, j * 128 : (j + 1) * 128].reshape(
                    4, ZC, 128
                )
        for slot in range(len(SLOTS)):
            fw(slot, g).start()
        after[:, pl.ds(z0, ZC), :] = aa[h].reshape(4, ZC, 512)
        xm[zone, pl.ds(z0, ZC), :] = mixin[h, zone // 4, lax.rem(zone, 4), pl.ds(z0, ZC), :]
        return carry

    lax.fori_loop(0, NG, step, 0)

    for n in (1, 2):
        src, own = pieces[n]
        pltpu.make_async_copy(src, own(zl), loc_sem.at[2 + n]).wait()
        for k in range(7):
            ag1(n, src, own, k).wait_recv()
    for k in range(15):
        ag2(1, own_i, k).start()
        ag2(2, own_o, k).start()

    locals_[1].wait()
    for slot in range(len(SLOTS)):
        remote(mixin.at[0, 0, 0], xm.at[zone], fw_s.at[slot], fw_r.at[slot], other).wait()

    def mixed(b):
        total = jnp.zeros((128, 128), F32)
        for k in range(3):
            weight = mx[b, k]
            live = jnp.where(k < degree[b], weight, jnp.zeros_like(weight))
            total += dot(live, xm[neighbours[k, b]])
        return total.astype(BF16)

    def block_of(o):
        return lax.rem(o // 8 + 1 + zone // 8, 2) * 8 + lax.rem(zone + o, 8)

    def back(o):
        b = block_of(o)
        return remote(stage.at[b], spat.at[zone], rt_s.at[o], rt_r.at[o], (tm, b))

    def send_back(o, carry):
        b = block_of(o)
        stage[b] = mixed(b)
        back(o).start()
        return carry

    lax.fori_loop(0, 8, send_back, 0)
    lax.fori_loop(9, 16, send_back, 0)
    spat[zone] = mixed(zone)

    for k in range(15):
        ag2(1, own_i, k).wait_recv()
        ag2(2, own_o, k).wait_recv()
    ag3(2, wi).start()
    ag3(3, wo).start()

    send_pat.wait_send()
    for g in range(NG):
        swap(g).wait_send()
        onward(g).wait_send()
        relay(g).wait_send()
    for k in range(7):
        ag1(0, src_kv, own_kv, k).wait_send()
        ag1(1, src_i, own_i, k).wait_send()
        ag1(2, src_o, own_o, k).wait_send()
        ag1(3, src_q, own_q, k).wait_send()
    for k in range(15):
        ag2(0, own_kv, k).wait_send()
        ag2(1, own_i, k).wait_send()
        ag2(2, own_o, k).wait_send()
        ag2(3, own_q, k).wait_send()
    ag3(0, wq).wait_send()
    ag3(1, wa).wait_send()
    ag3(2, wi).wait()
    ag3(3, wo).wait()

    wi2, wo2 = wi.reshape(512, 2048), wo.reshape(2048, 512)
    for turn in range(2):
        half = lax.rem(zone // 8 + turn, 2)
        for o in range(0, 8) if turn else range(9, 16):
            back(o).wait()
        for i in range(2):
            t = half * 2 + i
            wide = after[t] + jnp.concatenate(
                [spat[t * 4 + j].astype(F32) for j in range(4)], axis=1
            )
            acc[i * 128 : (i + 1) * 128, :] = wide
            nf[i * 128 : (i + 1) * 128, :] = rms(wide, g_ffn[...]).astype(BF16)
        for j in range(4):
            hidden = jax.nn.gelu(
                dot(nf[...], wi2[:, j * 512 : (j + 1) * 512]), approximate=True
            ).astype(BF16)
            acc[...] += dot(hidden, wo2[j * 512 : (j + 1) * 512, :])
        out[pl.ds(half * 2, 2)] = acc[...].astype(BF16).reshape(2, 128, 512)


def on_device(
    states, gain_attn, w_qkv, w_out_attn, pattern, gain_mix, neighbours, degree, mix, gain_ffn,
    w_in, w_out,
):
    hbm = pl.BlockSpec(memory_space=pl.ANY)
    vmem = pl.BlockSpec(memory_space=pltpu.VMEM)
    dma = pltpu.SemaphoreType.DMA
    return pl.pallas_call(
        kernel,
        out_shape=jax.ShapeDtypeStruct(states.shape, BF16),
        in_specs=[hbm] * 12,
        out_specs=vmem,
        scratch_shapes=[
            pltpu.VMEM((8, 256), F32),
            pltpu.VMEM((1, 512), F32),
            pltpu.VMEM((1, 512), F32),
            pltpu.VMEM((1, 512), F32),
            pltpu.SMEM((1, 2), jnp.int32),
            pltpu.SMEM((3, 16), jnp.int32),
            pltpu.SMEM((16,), jnp.int32),
            pltpu.VMEM((4, 4, 128, 512), BF16),
            pltpu.VMEM((8, 2, 2, 16, 1536), BF16),
            pltpu.VMEM((8, 2, 2, 16, 512), BF16),
            pltpu.VMEM((8, 2, 2, 16, 2048), BF16),
            pltpu.VMEM((8, 2, 8, 16, 512), BF16),
            pltpu.VMEM((16, 3, 128, 128), BF16),
            pltpu.VMEM((2, 8, 256), F32),
            pltpu.VMEM((4 * R, 512), BF16),
            pltpu.VMEM((4 * R, 1024), BF16),
            pltpu.VMEM((2 * R, 512), BF16),
            pltpu.VMEM((2 * R, 512), BF16),
            pltpu.VMEM((2, R, 512), F32),
            pltpu.VMEM((4, 128, 512), F32),
            pltpu.VMEM((2, 4, 4, 128, 128), BF16),
            pltpu.VMEM((16, 128, 128), BF16),
            pltpu.VMEM((16, 128, 128), BF16),
            pltpu.VMEM((16, 128, 128), BF16),
            pltpu.VMEM((256, 512), BF16),
            pltpu.VMEM((256, 512), F32),
            dma((12,)),
            dma((4, 7)), dma((4, 7)),
            dma((4, 15)), dma((4, 15)),
            dma((4,)), dma((4,)),
            dma((NG,)), dma((NG,)),
            dma, dma,
            dma((2, NG)), dma((2, NG)),
            dma((len(SLOTS),)), dma((len(SLOTS),)),
            dma((16,)), dma((16,)),
        ],
        compiler_params=pltpu.CompilerParams(
            collective_id=0, has_side_effects=True, vmem_limit_bytes=60 << 20
        ),
        cost_estimate=pl.CostEstimate(
            flops=5 * 10**9, bytes_accessed=8 * 10**6, transcendentals=2 * 10**6
        ),
        name="layer",
    )(
        states, w_qkv, w_out_attn, w_in, w_out, mix,
        gain_attn.reshape(1, -1), gain_mix.reshape(1, -1), gain_ffn.reshape(1, -1),
        pattern, neighbours.T, degree,
    )


def solution(mesh):
    return jax.shard_map(
        on_device,
        mesh=mesh,
        in_specs=(
            P("tm", "zone", None),
            P(),
            P("zone", None),
            P("zone", None),
            P("tm", None),
            P(),
            P(),
            P(),
            P(),
            P(),
            P("zone", None),
            P("zone", None),
        ),
        out_specs=P("tm", "zone", None),
        check_vma=False,
    )
```

```python
import functools

import jax
import jax.numpy as jnp
from jax import lax
from jax.experimental import pallas as pl
from jax.experimental.pallas import tpu as pltpu
from jax.sharding import PartitionSpec as P

MESH = pl.DeviceIdType.MESH
HEADS = 4
HD = 128
NG = 8
ZC = 16
R = 4 * ZC
F32, BF16 = jnp.float32, jnp.bfloat16

SLOTS = [(d, f) for d in (4, 3, -3, 2, -2, 1, -1, 0) for f in (0, 1) if (d, f) != (0, 0)]
RING = (-3, 3, 4, -2, 2, -1, 1)
XY = [(dx, dy) for dx in range(4) for dy in range(4) if dx or dy]


def rms(values, gain):
    mean_sq = jnp.mean(values * values, axis=-1, keepdims=True)
    return values * lax.rsqrt(mean_sq + 1e-06) * gain


def dot(a, b):
    return jnp.dot(a, b, preferred_element_type=F32)


def kernel(
    states, w_qkv, w_attn, w_in, w_out, mix, gains_a, gains_m, gains_f, pat_in, near_in, degree_in,
    out,
    pat, g_attn, g_mix, g_ffn, pattern, neighbours, degree, st, wq, wa, wi, wo, mx, pats, nrm, kv, qs, ctx, aa, after, mixin, xm, stage, spat, nf, acc, result,
    loc_sem, ag1_s, ag1_r, ag2_s, ag2_r, ag3_s, ag3_r, e1_s, e1_r, ep_s, ep_r, e2_s, e2_r,
    fw_s, fw_r, rt_s, rt_r,
):
    tm, zone = lax.axis_index("tm"), lax.axis_index("zone")
    h, col = lax.rem(tm, 2), tm // 2
    x, y = lax.rem(col, 4), col // 4
    zl, c = zone // 2, lax.rem(zone, 2)
    z = h * 8 + zl
    p = col

    def at_z(d, flip):
        zz = lax.rem(z + d + 16, 16)
        return (col * 2 + zz // 8, lax.rem(zz, 8) * 2 + lax.rem(c + flip, 2))

    def at_xy(dx, dy):
        xx, yy = lax.rem(x + dx, 4), lax.rem(y + dy, 4)
        return ((yy * 4 + xx) * 2 + h, zone)

    following = (lax.rem(col + 1, 16) * 2 + h, zone)
    partner = at_z(8, 0)
    other = at_z(0, 1)

    def remote(src, dst, ssem, rsem, dev):
        return pltpu.make_async_remote_copy(
            src, dst, ssem, rsem, device_id=dev, device_id_type=MESH
        )

    barrier = pltpu.get_barrier_semaphore()
    for d in sorted(range(16), key=lambda v: -min(v, 16 - v)):
        for f in (0, 1):
            if (d, f) != (0, 0):
                pl.semaphore_signal(barrier, inc=1, device_id=at_z(d, f), device_id_type=MESH)
    for dx, dy in XY:
        pl.semaphore_signal(barrier, inc=1, device_id=at_xy(dx, dy), device_id_type=MESH)
    locals_ = [
        pltpu.make_async_copy(states, st.at[2 + h], loc_sem.at[0]),
        pltpu.make_async_copy(mix, mx, loc_sem.at[1]),
        pltpu.make_async_copy(pat_in, pattern, loc_sem.at[6]),
        pltpu.make_async_copy(gains_a, g_attn, loc_sem.at[7]),
        pltpu.make_async_copy(gains_m, g_mix, loc_sem.at[8]),
        pltpu.make_async_copy(gains_f, g_ffn, loc_sem.at[9]),
        pltpu.make_async_copy(near_in, neighbours, loc_sem.at[10]),
        pltpu.make_async_copy(degree_in, degree, loc_sem.at[11]),
    ]
    r8, c8 = p // 8, pl.multiple_of(lax.rem(p, 8) * 128, 128)
    p8 = lax.rem(p, 8)
    r4, c4 = p8 // 4, pl.multiple_of(lax.rem(p8, 4) * 128, 128)
    i8 = pl.multiple_of(lax.rem(p, 8) * 256, 256)
    g2, h2 = p // 2, pl.multiple_of(lax.rem(p, 2) * 256, 256)
    first = p < 8

    src_kv = w_qkv.at[pl.ds(pl.multiple_of(r8 * 16, 16), 16), pl.ds(512 + c8, 128)]
    src_q = w_qkv.at[pl.ds(pl.multiple_of(r4 * 16, 16), 16), pl.ds(c4, 128)]
    src_a = w_attn.at[pl.ds(pl.multiple_of(r4 * 16, 16), 16), pl.ds(c4, 128)]
    src_i = w_in.at[pl.ds(pl.multiple_of(r8 * 16, 16), 16), pl.ds(i8, 256)]
    src_o = w_out.at[pl.ds(pl.multiple_of(g2 * 16, 16), 16), pl.ds(h2, 256)]

    def own_kv(zz):
        return wq.at[zz, c, r8, :, pl.ds(512 + c8, 128)]

    def own_q(zz):
        return wq.at[zz, c, r4, :, pl.ds(c4, 128)]

    def own_a(zz):
        return wa.at[zz, c, r4, :, pl.ds(c4, 128)]

    def own_i(zz):
        return wi.at[zz, c, r8, :, pl.ds(i8, 256)]

    def own_o(zz):
        return wo.at[zz, c, g2, :, pl.ds(h2, 256)]

    pieces = ((src_kv, own_kv), (src_i, own_i), (src_o, own_o))
    every = pl.ds(0, 8)

    for cp in locals_:
        cp.start()
    for n, (src, own) in enumerate(pieces):
        pltpu.make_async_copy(src, own(zl), loc_sem.at[2 + n]).start()

    @pl.when(first)
    def _():
        pltpu.make_async_copy(src_q, own_q(zl), loc_sem.at[5]).start()

    @pl.when(jnp.logical_not(first))
    def _():
        pltpu.make_async_copy(src_a, own_a(zl), loc_sem.at[5]).start()

    locals_[2].wait()
    upper = lax.broadcasted_iota(jnp.int32, (8, 256), 0) < 4
    pat[...] = jnp.where(upper, pattern[0, 0], pattern[0, 1]).astype(F32)
    pats[pl.ds(h, 1)] = pat[...].reshape(1, 8, 256)
    pl.semaphore_wait(barrier, 46)

    def chunk(ref, g):
        return ref.at[:, pl.ds(pl.multiple_of(g * ZC, ZC), ZC), :]

    def swap(g):
        return remote(chunk(states, g), chunk(st.at[2 + h], g), e1_s.at[g], e1_r.at[g], partner)

    def swapped(g):
        return remote(chunk(states, g), chunk(st.at[3 - h], g), e1_s.at[g], e1_r.at[g], partner)

    def onward(g):
        return remote(
            chunk(states, g), chunk(st.at[h], g), e2_s.at[0, g], e2_r.at[0, g], following
        )

    def relay(g):
        return remote(
            chunk(st.at[3 - h], g), chunk(st.at[1 - h], g), e2_s.at[1, g], e2_r.at[1, g], following
        )

    def ag1(n, src, own, k):
        return remote(src, own(zl), ag1_s.at[n, k], ag1_r.at[n, k], at_z(RING[k], 0))

    send_pat = remote(pat, pats.at[h], ep_s, ep_r, partner)
    for k in range(7):
        ag1(0, src_kv, own_kv, k).start()

    @pl.when(first)
    def _():
        for k in range(7):
            ag1(3, src_q, own_q, k).start()

    @pl.when(jnp.logical_not(first))
    def _():
        for k in range(7):
            ag1(3, src_a, own_a, k).start()

    send_pat.start()
    for g in range(NG):
        swap(g).start()
        if g == 3:
            for k in range(7):
                ag1(1, src_i, own_i, k).start()
                ag1(2, src_o, own_o, k).start()
        if g < 2:
            onward(g).start()

    def ag2(n, own, k):
        dev = at_xy((k + 1) // 4, lax.rem(k + 1, 4))
        return remote(own(every), own(every), ag2_s.at[n, k], ag2_r.at[n, k], dev)

    for n in (0, 3):
        src, own = pieces[0] if n == 0 else (src_q, own_q)
        pltpu.make_async_copy(src, own(zl), loc_sem.at[2 if n == 0 else 5]).wait()
        for k in range(7):
            ag1(n, src, own, k).wait_recv()
    for k in range(15):
        ag2(0, own_kv, k).start()

    @pl.when(first)
    def _():
        for k in range(15):
            ag2(3, own_q, k).start()

    @pl.when(jnp.logical_not(first))
    def _():
        for k in range(15):
            ag2(3, own_a, k).start()

    for g in range(2, NG):
        onward(g).start()
    for k in range(15):
        ag2(0, own_kv, k).wait_recv()
        ag2(3, own_q, k).wait_recv()

    def ag3(n, w):
        return remote(w.at[:, c], w.at[:, c], ag3_s.at[n], ag3_r.at[n], other)

    ag3(0, wq).start()
    ag3(1, wa).start()
    locals_[0].wait()
    for n in (3, 4, 5, 6, 7):
        locals_[n].wait()
    send_pat.wait_recv()
    ag3(0, wq).wait_recv()
    ag3(1, wa).wait_recv()
    wq2, wa2 = wq.reshape(512, 1536), wa.reshape(512, 512)

    rows = lax.broadcasted_iota(jnp.int32, (R, 3 * R), 0)
    cols = lax.broadcasted_iota(jnp.int32, (R, 3 * R), 1)
    same = lax.rem(rows, ZC) == lax.rem(cols, ZC)
    segment = cols // R
    causal = same & (segment == 2) & (lax.rem(cols, R) // ZC <= rows // ZC)
    back1, back2 = same & (segment == 1), same & (segment == 0)

    def fw(slot, g):
        d, f = SLOTS[slot]
        if d == 4:
            d = 4 - 8 * lax.rem(g, 2)
        zz = lax.rem(z + d + 16, 16)
        m = lax.rem(zz, 8) * 2 + lax.rem(c + f, 2)
        span = pl.ds(pl.multiple_of(g * ZC, ZC), ZC)
        return remote(
            mixin.at[zz // 8, m // 4, lax.rem(m, 4), span],
            xm.at[zone, span],
            fw_s.at[slot],
            fw_r.at[slot],
            at_z(d, f),
        )

    swapped(0).wait_recv()
    relay(0).start()

    def step(g, carry):
        z0 = pl.multiple_of(g * ZC, ZC)

        @pl.when(g + 1 < NG)
        def _():
            swapped(g + 1).wait_recv()
            relay(g + 1).start()

        @pl.when(g == NG - 2)
        def _():
            for n in (1, 2):
                src, own = pieces[n]
                pltpu.make_async_copy(src, own(zl), loc_sem.at[2 + n]).wait()
                for k in range(7):
                    ag1(n, src, own, k).wait_recv()
            for k in range(15):
                ag2(1, own_i, k).start()
                ag2(2, own_o, k).start()

        onward(g).wait_recv()
        relay(g).wait_recv()
        for b in range(4):
            block = st[b, :, pl.ds(z0, ZC), :].reshape(R, 512).astype(F32)
            nrm[b * R : (b + 1) * R, :] = rms(block, g_attn[...]).astype(BF16)
        for j in range(2):
            kv[:, j * 512 : (j + 1) * 512] = dot(
                nrm[...], wq2[:, (j + 1) * 512 : (j + 2) * 512]
            ).astype(BF16)
        qs[...] = dot(nrm[2 * R :, :], wq2[:, 0:512]).astype(BF16)
        pairs = [(t, hd) for t in range(2) for hd in range(HEADS)]
        scores = []
        for t, hd in pairs:
            q = qs[t * R : (t + 1) * R, hd * HD : (hd + 1) * HD]
            k = kv[t * R : (t + 3) * R, hd * HD : (hd + 1) * HD]
            scores.append(
                lax.dot_general(q, k, (((1,), (1,)), ((), ())), preferred_element_type=F32)
            )
        allowed = []
        for t in range(2):
            ok1 = jnp.where((col * 2 + t) >= 1, pats[t, 0:1, 0 : 3 * R], 0.0) > 0.5
            ok2 = jnp.where((col * 2 + t) >= 2, pats[t, 4:5, 0 : 3 * R], 0.0) > 0.5
            allowed.append(causal | (back1 & ok1) | (back2 & ok2))
        scores = [
            jnp.where(allowed[t], s * HD**-0.5, -1e30) for (t, _), s in zip(pairs, scores)
        ]
        tops = [jnp.max(s, axis=-1, keepdims=True) for s in scores]
        weights = [jnp.exp(s - top) for s, top in zip(scores, tops)]
        got = [
            dot(e.astype(BF16), kv[t * R : (t + 3) * R, 512 + hd * HD : 512 + (hd + 1) * HD])
            for (t, hd), e in zip(pairs, weights)
        ]
        totals = [jnp.sum(e, axis=-1, keepdims=True) for e in weights]
        for (t, hd), part, total in zip(pairs, got, totals):
            ctx[t * R : (t + 1) * R, hd * HD : (hd + 1) * HD] = (part / total).astype(BF16)
        both = dot(ctx[...], wa2[...])
        for t in range(2):
            block = st[2 + t, :, pl.ds(z0, ZC), :].reshape(R, 512).astype(F32)
            wide = block + both[t * R : (t + 1) * R, :]
            aa[t] = wide
            mi = rms(wide, g_mix[...]).astype(BF16)
            for j in range(4):
                mixin[t, :, j, pl.ds(z0, ZC), :] = mi[:, j * 128 : (j + 1) * 128].reshape(
                    4, ZC, 128
                )
        for slot in range(len(SLOTS)):
            fw(slot, g).start()
        after[:, pl.ds(z0, ZC), :] = aa[h].reshape(4, ZC, 512)
        xm[zone, pl.ds(z0, ZC), :] = mixin[h, zone // 4, lax.rem(zone, 4), pl.ds(z0, ZC), :]
        return carry

    lax.fori_loop(0, NG, step, 0)

    locals_[1].wait()
    for slot in range(len(SLOTS)):
        remote(mixin.at[0, 0, 0], xm.at[zone], fw_s.at[slot], fw_r.at[slot], other).wait()

    def mixed(b):
        total = jnp.zeros((128, 128), F32)
        for k in range(3):
            weight = mx[b, k]
            live = jnp.where(k < degree[b], weight, jnp.zeros_like(weight))
            total += dot(live, xm[neighbours[k, b]])
        return total.astype(BF16)

    def block_of(o):
        return lax.rem(o // 8 + 1 + zone // 8, 2) * 8 + lax.rem(zone + o, 8)

    def back(o):
        b = block_of(o)
        return remote(stage.at[b], spat.at[zone], rt_s.at[o], rt_r.at[o], (tm, b))

    def send_back(o, carry):
        b = block_of(o)
        stage[b] = mixed(b)
        back(o).start()
        return carry

    lax.fori_loop(0, 8, send_back, 0)
    lax.fori_loop(9, 16, send_back, 0)
    spat[zone] = mixed(zone)

    for k in range(15):
        ag2(1, own_i, k).wait_recv()
        ag2(2, own_o, k).wait_recv()
    ag3(2, wi).start()
    ag3(3, wo).start()

    send_pat.wait_send()
    for g in range(NG):
        swap(g).wait_send()
        onward(g).wait_send()
        relay(g).wait_send()
    for k in range(7):
        ag1(0, src_kv, own_kv, k).wait_send()
        ag1(1, src_i, own_i, k).wait_send()
        ag1(2, src_o, own_o, k).wait_send()
        ag1(3, src_q, own_q, k).wait_send()
    for k in range(15):
        ag2(0, own_kv, k).wait_send()
        ag2(1, own_i, k).wait_send()
        ag2(2, own_o, k).wait_send()
        ag2(3, own_q, k).wait_send()
    ag3(0, wq).wait_send()
    ag3(1, wa).wait_send()
    ag3(2, wi).wait()
    ag3(3, wo).wait()

    wi2, wo2 = wi.reshape(512, 2048), wo.reshape(2048, 512)
    written = []
    for turn in range(2):
        half = lax.rem(zone // 8 + turn, 2)
        for o in range(0, 8) if turn else range(9, 16):
            back(o).wait()
        for i in range(2):
            t = half * 2 + i
            wide = after[t] + jnp.concatenate(
                [spat[t * 4 + j].astype(F32) for j in range(4)], axis=1
            )
            acc[i * 128 : (i + 1) * 128, :] = wide
            nf[i * 128 : (i + 1) * 128, :] = rms(wide, g_ffn[...]).astype(BF16)
        for j in range(4):
            hidden = jax.nn.gelu(
                dot(nf[...], wi2[:, j * 512 : (j + 1) * 512]), approximate=True
            ).astype(BF16)
            acc[...] += dot(hidden, wo2[j * 512 : (j + 1) * 512, :])
        result[turn] = acc[...].astype(BF16).reshape(2, 128, 512)
        written.append(
            pltpu.make_async_copy(
                result.at[turn], out.at[pl.ds(half * 2, 2)], loc_sem.at[turn]
            )
        )
        written[turn].start()
    for cp in written:
        cp.wait()


def on_device(
    states, gain_attn, w_qkv, w_out_attn, pattern, gain_mix, neighbours, degree, mix, gain_ffn,
    w_in, w_out,
):
    hbm = pl.BlockSpec(memory_space=pl.ANY)
    dma = pltpu.SemaphoreType.DMA
    return pl.pallas_call(
        kernel,
        out_shape=jax.ShapeDtypeStruct(states.shape, BF16),
        in_specs=[hbm] * 12,
        out_specs=hbm,
        scratch_shapes=[
            pltpu.VMEM((8, 256), F32),
            pltpu.VMEM((1, 512), F32),
            pltpu.VMEM((1, 512), F32),
            pltpu.VMEM((1, 512), F32),
            pltpu.SMEM((1, 2), jnp.int32),
            pltpu.SMEM((3, 16), jnp.int32),
            pltpu.SMEM((16,), jnp.int32),
            pltpu.VMEM((4, 4, 128, 512), BF16),
            pltpu.VMEM((8, 2, 2, 16, 1536), BF16),
            pltpu.VMEM((8, 2, 2, 16, 512), BF16),
            pltpu.VMEM((8, 2, 2, 16, 2048), BF16),
            pltpu.VMEM((8, 2, 8, 16, 512), BF16),
            pltpu.VMEM((16, 3, 128, 128), BF16),
            pltpu.VMEM((2, 8, 256), F32),
            pltpu.VMEM((4 * R, 512), BF16),
            pltpu.VMEM((4 * R, 1024), BF16),
            pltpu.VMEM((2 * R, 512), BF16),
            pltpu.VMEM((2 * R, 512), BF16),
            pltpu.VMEM((2, R, 512), F32),
            pltpu.VMEM((4, 128, 512), F32),
            pltpu.VMEM((2, 4, 4, 128, 128), BF16),
            pltpu.VMEM((16, 128, 128), BF16),
            pltpu.VMEM((16, 128, 128), BF16),
            pltpu.VMEM((16, 128, 128), BF16),
            pltpu.VMEM((256, 512), BF16),
            pltpu.VMEM((256, 512), F32),
            pltpu.VMEM((2, 2, 128, 512), BF16),
            dma((12,)),
            dma((4, 7)), dma((4, 7)),
            dma((4, 15)), dma((4, 15)),
            dma((4,)), dma((4,)),
            dma((NG,)), dma((NG,)),
            dma, dma,
            dma((2, NG)), dma((2, NG)),
            dma((len(SLOTS),)), dma((len(SLOTS),)),
            dma((16,)), dma((16,)),
        ],
        compiler_params=pltpu.CompilerParams(
            collective_id=0, has_side_effects=True, vmem_limit_bytes=60 << 20
        ),
        cost_estimate=pl.CostEstimate(
            flops=5 * 10**9, bytes_accessed=8 * 10**6, transcendentals=2 * 10**6
        ),
        name="layer",
    )(
        states, w_qkv, w_out_attn, w_in, w_out, mix,
        gain_attn.reshape(1, -1), gain_mix.reshape(1, -1), gain_ffn.reshape(1, -1),
        pattern, neighbours.T, degree,
    )


def solution(mesh):
    return jax.shard_map(
        on_device,
        mesh=mesh,
        in_specs=(
            P("tm", "zone", None),
            P(),
            P("zone", None),
            P("zone", None),
            P("tm", None),
            P(),
            P(),
            P(),
            P(),
            P(),
            P("zone", None),
            P("zone", None),
        ),
        out_specs=P("tm", "zone", None),
        check_vma=False,
    )
```

```python
import functools

import jax
import jax.numpy as jnp
from jax import lax
from jax.experimental import pallas as pl
from jax.experimental.pallas import tpu as pltpu
from jax.sharding import PartitionSpec as P

MESH = pl.DeviceIdType.MESH
HEADS = 4
HD = 128
NG = 8
ZC = 16
R = 4 * ZC
HELD = 6
F32, BF16 = jnp.float32, jnp.bfloat16

SLOTS = [(d, f) for d in (4, 3, -3, 2, -2, 1, -1, 0) for f in (0, 1) if (d, f) != (0, 0)]
RING = (-3, 3, 4, -2, 2, -1, 1)
XY = [(dx, dy) for dx in range(4) for dy in range(4) if dx or dy]


def rms(values, gain):
    mean_sq = jnp.mean(values * values, axis=-1, keepdims=True)
    return values * lax.rsqrt(mean_sq + 1e-06) * gain


def dot(a, b):
    return jnp.dot(a, b, preferred_element_type=F32)


def kernel(
    states, w_qkv, w_attn, w_in, w_out, mix, gains_a, gains_m, gains_f, pat_in, near_in, degree_in,
    out,
    pat, g_attn, g_mix, g_ffn, pattern, neighbours, degree, st, wq, wa, wi, wo, mx, pats, nrm, kv, qs, ctx, aa, after, mixin, xm, stage, spat, nf, acc, result,
    loc_sem, ag1_s, ag1_r, ag2_s, ag2_r, ag3_s, ag3_r, e1_s, e1_r, ep_s, ep_r, e2_s, e2_r,
    fw_s, fw_r, rt_s, rt_r,
):
    tm, zone = lax.axis_index("tm"), lax.axis_index("zone")
    h, col = lax.rem(tm, 2), tm // 2
    x, y = lax.rem(col, 4), col // 4
    zl, c = zone // 2, lax.rem(zone, 2)
    z = h * 8 + zl
    p = col

    def at_z(d, flip):
        zz = lax.rem(z + d + 16, 16)
        return (col * 2 + zz // 8, lax.rem(zz, 8) * 2 + lax.rem(c + flip, 2))

    def at_xy(dx, dy):
        xx, yy = lax.rem(x + dx, 4), lax.rem(y + dy, 4)
        return ((yy * 4 + xx) * 2 + h, zone)

    following = (lax.rem(col + 1, 16) * 2 + h, zone)
    partner = at_z(8, 0)
    other = at_z(0, 1)

    def remote(src, dst, ssem, rsem, dev):
        return pltpu.make_async_remote_copy(
            src, dst, ssem, rsem, device_id=dev, device_id_type=MESH
        )

    barrier = pltpu.get_barrier_semaphore()
    for d in sorted(range(16), key=lambda v: -min(v, 16 - v)):
        for f in (0, 1):
            if (d, f) != (0, 0):
                pl.semaphore_signal(barrier, inc=1, device_id=at_z(d, f), device_id_type=MESH)
    for dx, dy in XY:
        pl.semaphore_signal(barrier, inc=1, device_id=at_xy(dx, dy), device_id_type=MESH)
    locals_ = [
        pltpu.make_async_copy(states, st.at[2 + h], loc_sem.at[0]),
        pltpu.make_async_copy(mix, mx, loc_sem.at[1]),
        pltpu.make_async_copy(pat_in, pattern, loc_sem.at[6]),
        pltpu.make_async_copy(gains_a, g_attn, loc_sem.at[7]),
        pltpu.make_async_copy(gains_m, g_mix, loc_sem.at[8]),
        pltpu.make_async_copy(gains_f, g_ffn, loc_sem.at[9]),
        pltpu.make_async_copy(near_in, neighbours, loc_sem.at[10]),
        pltpu.make_async_copy(degree_in, degree, loc_sem.at[11]),
    ]
    r8, c8 = p // 8, pl.multiple_of(lax.rem(p, 8) * 128, 128)
    p8 = lax.rem(p, 8)
    r4, c4 = p8 // 4, pl.multiple_of(lax.rem(p8, 4) * 128, 128)
    i8 = pl.multiple_of(lax.rem(p, 8) * 256, 256)
    g2, h2 = p // 2, pl.multiple_of(lax.rem(p, 2) * 256, 256)
    first = p < 8

    src_kv = w_qkv.at[pl.ds(pl.multiple_of(r8 * 16, 16), 16), pl.ds(512 + c8, 128)]
    src_q = w_qkv.at[pl.ds(pl.multiple_of(r4 * 16, 16), 16), pl.ds(c4, 128)]
    src_a = w_attn.at[pl.ds(pl.multiple_of(r4 * 16, 16), 16), pl.ds(c4, 128)]
    src_i = w_in.at[pl.ds(pl.multiple_of(r8 * 16, 16), 16), pl.ds(i8, 256)]
    src_o = w_out.at[pl.ds(pl.multiple_of(g2 * 16, 16), 16), pl.ds(h2, 256)]

    def own_kv(zz):
        return wq.at[zz, c, r8, :, pl.ds(512 + c8, 128)]

    def own_q(zz):
        return wq.at[zz, c, r4, :, pl.ds(c4, 128)]

    def own_a(zz):
        return wa.at[zz, c, r4, :, pl.ds(c4, 128)]

    def own_i(zz):
        return wi.at[zz, c, r8, :, pl.ds(i8, 256)]

    def own_o(zz):
        return wo.at[zz, c, g2, :, pl.ds(h2, 256)]

    pieces = ((src_kv, own_kv), (src_i, own_i), (src_o, own_o))
    every = pl.ds(0, 8)

    for cp in locals_:
        cp.start()
    for n, (src, own) in enumerate(pieces):
        pltpu.make_async_copy(src, own(zl), loc_sem.at[2 + n]).start()

    @pl.when(first)
    def _():
        pltpu.make_async_copy(src_q, own_q(zl), loc_sem.at[5]).start()

    @pl.when(jnp.logical_not(first))
    def _():
        pltpu.make_async_copy(src_a, own_a(zl), loc_sem.at[5]).start()

    locals_[2].wait()
    upper = lax.broadcasted_iota(jnp.int32, (8, 256), 0) < 4
    pat[...] = jnp.where(upper, pattern[0, 0], pattern[0, 1]).astype(F32)
    pats[pl.ds(h, 1)] = pat[...].reshape(1, 8, 256)
    pl.semaphore_wait(barrier, 46)

    def chunk(ref, g):
        return ref.at[:, pl.ds(pl.multiple_of(g * ZC, ZC), ZC), :]

    def swap(g):
        return remote(chunk(states, g), chunk(st.at[2 + h], g), e1_s.at[g], e1_r.at[g], partner)

    def swapped(g):
        return remote(chunk(states, g), chunk(st.at[3 - h], g), e1_s.at[g], e1_r.at[g], partner)

    def onward(g):
        return remote(
            chunk(states, g), chunk(st.at[h], g), e2_s.at[0, g], e2_r.at[0, g], following
        )

    def relay(g):
        return remote(
            chunk(st.at[3 - h], g), chunk(st.at[1 - h], g), e2_s.at[1, g], e2_r.at[1, g], following
        )

    def ag1(n, src, own, k):
        return remote(src, own(zl), ag1_s.at[n, k], ag1_r.at[n, k], at_z(RING[k], 0))

    send_pat = remote(pat, pats.at[h], ep_s, ep_r, partner)
    send_pat.start()
    swap(0).start()
    onward(0).start()
    for k in range(7):
        ag1(0, src_kv, own_kv, k).start()

    @pl.when(first)
    def _():
        for k in range(7):
            ag1(3, src_q, own_q, k).start()

    @pl.when(jnp.logical_not(first))
    def _():
        for k in range(7):
            ag1(3, src_a, own_a, k).start()

    for g in range(1, NG):
        swap(g).start()
        if g == 3:
            for k in range(7):
                ag1(1, src_i, own_i, k).start()
                ag1(2, src_o, own_o, k).start()
        if g < 2:
            onward(g).start()

    def ag2(n, own, k):
        dev = at_xy((k + 1) // 4, lax.rem(k + 1, 4))
        return remote(own(every), own(every), ag2_s.at[n, k], ag2_r.at[n, k], dev)

    for n in (0, 3):
        src, own = pieces[0] if n == 0 else (src_q, own_q)
        pltpu.make_async_copy(src, own(zl), loc_sem.at[2 if n == 0 else 5]).wait()
        for k in range(7):
            ag1(n, src, own, k).wait_recv()
    for k in range(15):
        ag2(0, own_kv, k).start()

    @pl.when(first)
    def _():
        for k in range(15):
            ag2(3, own_q, k).start()

    @pl.when(jnp.logical_not(first))
    def _():
        for k in range(15):
            ag2(3, own_a, k).start()

    for g in range(2, NG):
        onward(g).start()
    for k in range(15):
        ag2(0, own_kv, k).wait_recv()
        ag2(3, own_q, k).wait_recv()

    def ag3(n, w):
        return remote(w.at[:, c], w.at[:, c], ag3_s.at[n], ag3_r.at[n], other)

    ag3(0, wq).start()
    ag3(1, wa).start()
    locals_[0].wait()
    for n in (3, 4, 5, 6, 7):
        locals_[n].wait()
    send_pat.wait_recv()
    ag3(0, wq).wait_recv()
    ag3(1, wa).wait_recv()
    wq2, wa2 = wq.reshape(512, 1536), wa.reshape(512, 512)

    rows = lax.broadcasted_iota(jnp.int32, (R, 3 * R), 0)
    cols = lax.broadcasted_iota(jnp.int32, (R, 3 * R), 1)
    same = lax.rem(rows, ZC) == lax.rem(cols, ZC)
    segment = cols // R
    causal = same & (segment == 2) & (lax.rem(cols, R) // ZC <= rows // ZC)
    back1, back2 = same & (segment == 1), same & (segment == 0)

    def fw(slot, d, low, count):
        f = SLOTS[slot][1]
        zz = lax.rem(z + d + 16, 16)
        m = lax.rem(zz, 8) * 2 + lax.rem(c + f, 2)
        span = pl.ds(low, count)
        return remote(
            mixin.at[zz // 8, m // 4, lax.rem(m, 4), span],
            xm.at[zone, span],
            fw_s.at[slot],
            fw_r.at[slot],
            at_z(d, f),
        )

    def send_held():
        for slot, (d, f) in enumerate(SLOTS):
            if d == 4:
                fw(slot, 4, 0, HELD * ZC // 2).start()
                fw(slot, -4, HELD * ZC // 2, HELD * ZC // 2).start()
            else:
                fw(slot, d, 0, HELD * ZC).start()

    def send_chunk(g):
        for slot, (d, f) in enumerate(SLOTS):
            way = 4 - 8 * lax.rem(g, 2) if d == 4 else d
            fw(slot, way, pl.multiple_of(g * ZC, ZC), ZC).start()

    swapped(0).wait_recv()
    relay(0).start()

    def step(g, carry):
        z0 = pl.multiple_of(g * ZC, ZC)

        @pl.when(g + 1 < NG)
        def _():
            swapped(g + 1).wait_recv()
            relay(g + 1).start()

        @pl.when(g == HELD)
        def _():
            send_held()

        @pl.when(g == NG - 2)
        def _():
            for n in (1, 2):
                src, own = pieces[n]
                pltpu.make_async_copy(src, own(zl), loc_sem.at[2 + n]).wait()
                for k in range(7):
                    ag1(n, src, own, k).wait_recv()
            for k in range(15):
                ag2(1, own_i, k).start()
                ag2(2, own_o, k).start()

        onward(g).wait_recv()
        relay(g).wait_recv()
        for b in range(4):
            block = st[b, :, pl.ds(z0, ZC), :].reshape(R, 512).astype(F32)
            nrm[b * R : (b + 1) * R, :] = rms(block, g_attn[...]).astype(BF16)
        for j in range(2):
            kv[:, j * 512 : (j + 1) * 512] = dot(
                nrm[...], wq2[:, (j + 1) * 512 : (j + 2) * 512]
            ).astype(BF16)
        qs[...] = dot(nrm[2 * R :, :], wq2[:, 0:512]).astype(BF16)
        pairs = [(t, hd) for t in range(2) for hd in range(HEADS)]
        scores = []
        for t, hd in pairs:
            q = qs[t * R : (t + 1) * R, hd * HD : (hd + 1) * HD]
            k = kv[t * R : (t + 3) * R, hd * HD : (hd + 1) * HD]
            scores.append(
                lax.dot_general(q, k, (((1,), (1,)), ((), ())), preferred_element_type=F32)
            )
        allowed = []
        for t in range(2):
            ok1 = jnp.where((col * 2 + t) >= 1, pats[t, 0:1, 0 : 3 * R], 0.0) > 0.5
            ok2 = jnp.where((col * 2 + t) >= 2, pats[t, 4:5, 0 : 3 * R], 0.0) > 0.5
            allowed.append(causal | (back1 & ok1) | (back2 & ok2))
        scores = [
            jnp.where(allowed[t], s * HD**-0.5, -1e30) for (t, _), s in zip(pairs, scores)
        ]
        tops = [jnp.max(s, axis=-1, keepdims=True) for s in scores]
        weights = [jnp.exp(s - top) for s, top in zip(scores, tops)]
        got = [
            dot(e.astype(BF16), kv[t * R : (t + 3) * R, 512 + hd * HD : 512 + (hd + 1) * HD])
            for (t, hd), e in zip(pairs, weights)
        ]
        totals = [jnp.sum(e, axis=-1, keepdims=True) for e in weights]
        for (t, hd), part, total in zip(pairs, got, totals):
            ctx[t * R : (t + 1) * R, hd * HD : (hd + 1) * HD] = (part / total).astype(BF16)
        both = dot(ctx[...], wa2[...])
        for t in range(2):
            block = st[2 + t, :, pl.ds(z0, ZC), :].reshape(R, 512).astype(F32)
            wide = block + both[t * R : (t + 1) * R, :]
            aa[t] = wide
            mi = rms(wide, g_mix[...]).astype(BF16)
            for j in range(4):
                mixin[t, :, j, pl.ds(z0, ZC), :] = mi[:, j * 128 : (j + 1) * 128].reshape(
                    4, ZC, 128
                )
        @pl.when(g >= HELD)
        def _():
            send_chunk(g)

        after[:, pl.ds(z0, ZC), :] = aa[h].reshape(4, ZC, 512)
        xm[zone, pl.ds(z0, ZC), :] = mixin[h, zone // 4, lax.rem(zone, 4), pl.ds(z0, ZC), :]
        return carry

    lax.fori_loop(0, NG, step, 0)

    locals_[1].wait()
    for slot in range(len(SLOTS)):
        remote(mixin.at[0, 0, 0], xm.at[zone], fw_s.at[slot], fw_r.at[slot], other).wait()

    def mixed(b):
        total = jnp.zeros((128, 128), F32)
        for k in range(3):
            weight = mx[b, k]
            live = jnp.where(k < degree[b], weight, jnp.zeros_like(weight))
            total += dot(live, xm[neighbours[k, b]])
        return total.astype(BF16)

    def block_of(o):
        return lax.rem(o // 8 + 1 + zone // 8, 2) * 8 + lax.rem(zone + o, 8)

    def back(o):
        b = block_of(o)
        return remote(stage.at[b], spat.at[zone], rt_s.at[o], rt_r.at[o], (tm, b))

    def send_back(o, carry):
        b = block_of(o)
        stage[b] = mixed(b)
        back(o).start()
        return carry

    lax.fori_loop(0, 8, send_back, 0)
    lax.fori_loop(9, 16, send_back, 0)
    spat[zone] = mixed(zone)

    for k in range(15):
        ag2(1, own_i, k).wait_recv()
        ag2(2, own_o, k).wait_recv()
    ag3(2, wi).start()
    ag3(3, wo).start()

    send_pat.wait_send()
    for g in range(NG):
        swap(g).wait_send()
        onward(g).wait_send()
        relay(g).wait_send()
    for k in range(7):
        ag1(0, src_kv, own_kv, k).wait_send()
        ag1(1, src_i, own_i, k).wait_send()
        ag1(2, src_o, own_o, k).wait_send()
        ag1(3, src_q, own_q, k).wait_send()
    for k in range(15):
        ag2(0, own_kv, k).wait_send()
        ag2(1, own_i, k).wait_send()
        ag2(2, own_o, k).wait_send()
        ag2(3, own_q, k).wait_send()
    ag3(0, wq).wait_send()
    ag3(1, wa).wait_send()
    ag3(2, wi).wait()
    ag3(3, wo).wait()

    wi2, wo2 = wi.reshape(512, 2048), wo.reshape(2048, 512)
    written = []
    for turn in range(2):
        half = lax.rem(zone // 8 + turn, 2)
        for o in range(0, 8) if turn else range(9, 16):
            back(o).wait()
        for i in range(2):
            t = half * 2 + i
            wide = after[t] + jnp.concatenate(
                [spat[t * 4 + j].astype(F32) for j in range(4)], axis=1
            )
            acc[i * 128 : (i + 1) * 128, :] = wide
            nf[i * 128 : (i + 1) * 128, :] = rms(wide, g_ffn[...]).astype(BF16)
        for j in range(4):
            hidden = jax.nn.gelu(
                dot(nf[...], wi2[:, j * 512 : (j + 1) * 512]), approximate=True
            ).astype(BF16)
            acc[...] += dot(hidden, wo2[j * 512 : (j + 1) * 512, :])
        result[turn] = acc[...].astype(BF16).reshape(2, 128, 512)
        written.append(
            pltpu.make_async_copy(
                result.at[turn], out.at[pl.ds(half * 2, 2)], loc_sem.at[turn]
            )
        )
        written[turn].start()
    for cp in written:
        cp.wait()


def on_device(
    states, gain_attn, w_qkv, w_out_attn, pattern, gain_mix, neighbours, degree, mix, gain_ffn,
    w_in, w_out,
):
    hbm = pl.BlockSpec(memory_space=pl.ANY)
    dma = pltpu.SemaphoreType.DMA
    return pl.pallas_call(
        kernel,
        out_shape=jax.ShapeDtypeStruct(states.shape, BF16),
        in_specs=[hbm] * 12,
        out_specs=hbm,
        scratch_shapes=[
            pltpu.VMEM((8, 256), F32),
            pltpu.VMEM((1, 512), F32),
            pltpu.VMEM((1, 512), F32),
            pltpu.VMEM((1, 512), F32),
            pltpu.SMEM((1, 2), jnp.int32),
            pltpu.SMEM((3, 16), jnp.int32),
            pltpu.SMEM((16,), jnp.int32),
            pltpu.VMEM((4, 4, 128, 512), BF16),
            pltpu.VMEM((8, 2, 2, 16, 1536), BF16),
            pltpu.VMEM((8, 2, 2, 16, 512), BF16),
            pltpu.VMEM((8, 2, 2, 16, 2048), BF16),
            pltpu.VMEM((8, 2, 8, 16, 512), BF16),
            pltpu.VMEM((16, 3, 128, 128), BF16),
            pltpu.VMEM((2, 8, 256), F32),
            pltpu.VMEM((4 * R, 512), BF16),
            pltpu.VMEM((4 * R, 1024), BF16),
            pltpu.VMEM((2 * R, 512), BF16),
            pltpu.VMEM((2 * R, 512), BF16),
            pltpu.VMEM((2, R, 512), F32),
            pltpu.VMEM((4, 128, 512), F32),
            pltpu.VMEM((2, 4, 4, 128, 128), BF16),
            pltpu.VMEM((16, 128, 128), BF16),
            pltpu.VMEM((16, 128, 128), BF16),
            pltpu.VMEM((16, 128, 128), BF16),
            pltpu.VMEM((256, 512), BF16),
            pltpu.VMEM((256, 512), F32),
            pltpu.VMEM((2, 2, 128, 512), BF16),
            dma((12,)),
            dma((4, 7)), dma((4, 7)),
            dma((4, 15)), dma((4, 15)),
            dma((4,)), dma((4,)),
            dma((NG,)), dma((NG,)),
            dma, dma,
            dma((2, NG)), dma((2, NG)),
            dma((len(SLOTS),)), dma((len(SLOTS),)),
            dma((16,)), dma((16,)),
        ],
        compiler_params=pltpu.CompilerParams(
            collective_id=0, has_side_effects=True, vmem_limit_bytes=60 << 20
        ),
        cost_estimate=pl.CostEstimate(
            flops=5 * 10**9, bytes_accessed=8 * 10**6, transcendentals=2 * 10**6
        ),
        name="layer",
    )(
        states, w_qkv, w_out_attn, w_in, w_out, mix,
        gain_attn.reshape(1, -1), gain_mix.reshape(1, -1), gain_ffn.reshape(1, -1),
        pattern, neighbours.T, degree,
    )


def solution(mesh):
    return jax.shard_map(
        on_device,
        mesh=mesh,
        in_specs=(
            P("tm", "zone", None),
            P(),
            P("zone", None),
            P("zone", None),
            P("tm", None),
            P(),
            P(),
            P(),
            P(),
            P(),
            P("zone", None),
            P("zone", None),
        ),
        out_specs=P("tm", "zone", None),
        check_vma=False,
    )
```

```python
import functools

import jax
import jax.numpy as jnp
from jax import lax
from jax.experimental import pallas as pl
from jax.experimental.pallas import tpu as pltpu
from jax.sharding import PartitionSpec as P

MESH = pl.DeviceIdType.MESH
HEADS = 4
HD = 128
NG = 8
ZC = 16
R = 4 * ZC
HELD = 6
F32, BF16 = jnp.float32, jnp.bfloat16

SLOTS = [(d, f) for d in (4, 3, -3, 2, -2, 1, -1, 0) for f in (0, 1) if (d, f) != (0, 0)]
RING = (-3, 3, 4, -2, 2, -1, 1)
XY = [(dx, dy) for dx in range(4) for dy in range(4) if dx or dy]


def rms(values, gain):
    mean_sq = jnp.mean(values * values, axis=-1, keepdims=True)
    return values * lax.rsqrt(mean_sq + 1e-06) * gain


def dot(a, b):
    return jnp.dot(a, b, preferred_element_type=F32)


def kernel(
    states, w_qkv, w_attn, w_in, w_out, mix, gains_a, gains_m, gains_f, pat_in, near_in, degree_in,
    out,
    pat, g_attn, g_mix, g_ffn, pattern, neighbours, degree, st, wq, wa, wi, wo, mx, pats, nrm, kv, qs, ctx, aa, after, mixin, xm, stage, spat, nf, acc, result,
    loc_sem, ag1_s, ag1_r, ag2_s, ag2_r, ag3_s, ag3_r, e1_s, e1_r, ep_s, ep_r, e2_s, e2_r,
    fw_s, fw_r, rt_s, rt_r,
):
    tm, zone = lax.axis_index("tm"), lax.axis_index("zone")
    h, col = lax.rem(tm, 2), tm // 2
    x, y = lax.rem(col, 4), col // 4
    zl, c = zone // 2, lax.rem(zone, 2)
    z = h * 8 + zl
    p = col

    def at_z(d, flip):
        zz = lax.rem(z + d + 16, 16)
        return (col * 2 + zz // 8, lax.rem(zz, 8) * 2 + lax.rem(c + flip, 2))

    def at_xy(dx, dy):
        xx, yy = lax.rem(x + dx, 4), lax.rem(y + dy, 4)
        return ((yy * 4 + xx) * 2 + h, zone)

    following = (lax.rem(col + 1, 16) * 2 + h, zone)
    partner = at_z(8, 0)
    other = at_z(0, 1)

    def remote(src, dst, ssem, rsem, dev):
        return pltpu.make_async_remote_copy(
            src, dst, ssem, rsem, device_id=dev, device_id_type=MESH
        )

    barrier = pltpu.get_barrier_semaphore()
    for d in sorted(range(16), key=lambda v: -min(v, 16 - v)):
        for f in (0, 1):
            if (d, f) != (0, 0):
                pl.semaphore_signal(barrier, inc=1, device_id=at_z(d, f), device_id_type=MESH)
    for dx, dy in XY:
        pl.semaphore_signal(barrier, inc=1, device_id=at_xy(dx, dy), device_id_type=MESH)
    locals_ = [
        pltpu.make_async_copy(states, st.at[2 + h], loc_sem.at[0]),
        pltpu.make_async_copy(mix, mx, loc_sem.at[1]),
        pltpu.make_async_copy(pat_in, pattern, loc_sem.at[6]),
        pltpu.make_async_copy(gains_a, g_attn, loc_sem.at[7]),
        pltpu.make_async_copy(gains_m, g_mix, loc_sem.at[8]),
        pltpu.make_async_copy(gains_f, g_ffn, loc_sem.at[9]),
        pltpu.make_async_copy(near_in, neighbours, loc_sem.at[10]),
        pltpu.make_async_copy(degree_in, degree, loc_sem.at[11]),
    ]
    r8, c8 = p // 8, pl.multiple_of(lax.rem(p, 8) * 128, 128)
    p8 = lax.rem(p, 8)
    r4, c4 = p8 // 4, pl.multiple_of(lax.rem(p8, 4) * 128, 128)
    i8 = pl.multiple_of(lax.rem(p, 8) * 256, 256)
    g2, h2 = p // 2, pl.multiple_of(lax.rem(p, 2) * 256, 256)
    first = p < 8

    src_kv = w_qkv.at[pl.ds(pl.multiple_of(r8 * 16, 16), 16), pl.ds(512 + c8, 128)]
    src_q = w_qkv.at[pl.ds(pl.multiple_of(r4 * 16, 16), 16), pl.ds(c4, 128)]
    src_a = w_attn.at[pl.ds(pl.multiple_of(r4 * 16, 16), 16), pl.ds(c4, 128)]
    src_i = w_in.at[pl.ds(pl.multiple_of(r8 * 16, 16), 16), pl.ds(i8, 256)]
    src_o = w_out.at[pl.ds(pl.multiple_of(g2 * 16, 16), 16), pl.ds(h2, 256)]

    def own_kv(zz):
        return wq.at[zz, c, r8, :, pl.ds(512 + c8, 128)]

    def own_q(zz):
        return wq.at[zz, c, r4, :, pl.ds(c4, 128)]

    def own_a(zz):
        return wa.at[zz, c, r4, :, pl.ds(c4, 128)]

    def own_i(zz):
        return wi.at[zz, c, r8, :, pl.ds(i8, 256)]

    def own_o(zz):
        return wo.at[zz, c, g2, :, pl.ds(h2, 256)]

    pieces = ((src_kv, own_kv), (src_i, own_i), (src_o, own_o))
    every = pl.ds(0, 8)

    for cp in locals_:
        cp.start()
    for n, (src, own) in enumerate(pieces):
        pltpu.make_async_copy(src, own(zl), loc_sem.at[2 + n]).start()

    @pl.when(first)
    def _():
        pltpu.make_async_copy(src_q, own_q(zl), loc_sem.at[5]).start()

    @pl.when(jnp.logical_not(first))
    def _():
        pltpu.make_async_copy(src_a, own_a(zl), loc_sem.at[5]).start()

    locals_[2].wait()
    upper = lax.broadcasted_iota(jnp.int32, (8, 256), 0) < 4
    pat[...] = jnp.where(upper, pattern[0, 0], pattern[0, 1]).astype(F32)
    pats[pl.ds(h, 1)] = pat[...].reshape(1, 8, 256)
    pl.semaphore_wait(barrier, 46)

    def chunk(ref, g):
        return ref.at[:, pl.ds(pl.multiple_of(g * ZC, ZC), ZC), :]

    def swap(g):
        return remote(chunk(states, g), chunk(st.at[2 + h], g), e1_s.at[g], e1_r.at[g], partner)

    def swapped(g):
        return remote(chunk(states, g), chunk(st.at[3 - h], g), e1_s.at[g], e1_r.at[g], partner)

    def onward(g):
        return remote(
            chunk(states, g), chunk(st.at[h], g), e2_s.at[0, g], e2_r.at[0, g], following
        )

    def relay(g):
        return remote(
            chunk(st.at[3 - h], g), chunk(st.at[1 - h], g), e2_s.at[1, g], e2_r.at[1, g], following
        )

    def ag1(n, src, own, k):
        return remote(src, own(zl), ag1_s.at[n, k], ag1_r.at[n, k], at_z(RING[k], 0))

    send_pat = remote(pat, pats.at[h], ep_s, ep_r, partner)
    send_pat.start()
    swap(0).start()
    onward(0).start()
    for k in range(7):
        ag1(0, src_kv, own_kv, k).start()

    @pl.when(first)
    def _():
        for k in range(7):
            ag1(3, src_q, own_q, k).start()

    @pl.when(jnp.logical_not(first))
    def _():
        for k in range(7):
            ag1(3, src_a, own_a, k).start()

    for g in range(1, NG):
        swap(g).start()
        if g == 3:
            for k in range(7):
                ag1(1, src_i, own_i, k).start()
                ag1(2, src_o, own_o, k).start()
        if g < 2:
            onward(g).start()

    def ag2(n, own, k):
        dev = at_xy((k + 1) // 4, lax.rem(k + 1, 4))
        return remote(own(every), own(every), ag2_s.at[n, k], ag2_r.at[n, k], dev)

    for n in (0, 3):
        src, own = pieces[0] if n == 0 else (src_q, own_q)
        pltpu.make_async_copy(src, own(zl), loc_sem.at[2 if n == 0 else 5]).wait()
        for k in range(7):
            ag1(n, src, own, k).wait_recv()
        if n == 0:
            for k in range(15):
                ag2(0, own_kv, k).start()

    @pl.when(first)
    def _():
        for k in range(15):
            ag2(3, own_q, k).start()

    @pl.when(jnp.logical_not(first))
    def _():
        for k in range(15):
            ag2(3, own_a, k).start()

    for g in range(2, NG):
        onward(g).start()
    for k in range(15):
        ag2(0, own_kv, k).wait_recv()
        ag2(3, own_q, k).wait_recv()

    def ag3(n, w):
        return remote(w.at[:, c], w.at[:, c], ag3_s.at[n], ag3_r.at[n], other)

    ag3(0, wq).start()
    ag3(1, wa).start()
    swapped(0).wait_recv()
    relay(0).start()
    locals_[0].wait()
    for n in (3, 4, 5, 6, 7):
        locals_[n].wait()
    send_pat.wait_recv()
    ag3(0, wq).wait_recv()
    ag3(1, wa).wait_recv()
    wq2, wa2 = wq.reshape(512, 1536), wa.reshape(512, 512)

    rows = lax.broadcasted_iota(jnp.int32, (R, 3 * R), 0)
    cols = lax.broadcasted_iota(jnp.int32, (R, 3 * R), 1)
    same = lax.rem(rows, ZC) == lax.rem(cols, ZC)
    segment = cols // R
    causal = same & (segment == 2) & (lax.rem(cols, R) // ZC <= rows // ZC)
    back1, back2 = same & (segment == 1), same & (segment == 0)

    def fw(slot, d, low, count):
        f = SLOTS[slot][1]
        zz = lax.rem(z + d + 16, 16)
        m = lax.rem(zz, 8) * 2 + lax.rem(c + f, 2)
        span = pl.ds(low, count)
        return remote(
            mixin.at[zz // 8, m // 4, lax.rem(m, 4), span],
            xm.at[zone, span],
            fw_s.at[slot],
            fw_r.at[slot],
            at_z(d, f),
        )

    def send_held():
        for slot, (d, f) in enumerate(SLOTS):
            if d == 4:
                fw(slot, 4, 0, HELD * ZC // 2).start()
                fw(slot, -4, HELD * ZC // 2, HELD * ZC // 2).start()
            else:
                fw(slot, d, 0, HELD * ZC).start()

    def send_chunk(g):
        for slot, (d, f) in enumerate(SLOTS):
            way = 4 - 8 * lax.rem(g, 2) if d == 4 else d
            fw(slot, way, pl.multiple_of(g * ZC, ZC), ZC).start()


    def step(g, carry):
        z0 = pl.multiple_of(g * ZC, ZC)

        @pl.when(g + 1 < NG)
        def _():
            swapped(g + 1).wait_recv()
            relay(g + 1).start()

        @pl.when(g == HELD)
        def _():
            send_held()

        @pl.when(g == NG - 2)
        def _():
            for n in (1, 2):
                src, own = pieces[n]
                pltpu.make_async_copy(src, own(zl), loc_sem.at[2 + n]).wait()
                for k in range(7):
                    ag1(n, src, own, k).wait_recv()
            for k in range(15):
                ag2(1, own_i, k).start()
                ag2(2, own_o, k).start()

        onward(g).wait_recv()
        relay(g).wait_recv()
        for b in range(4):
            block = st[b, :, pl.ds(z0, ZC), :].reshape(R, 512).astype(F32)
            nrm[b * R : (b + 1) * R, :] = rms(block, g_attn[...]).astype(BF16)
        for j in range(2):
            kv[:, j * 512 : (j + 1) * 512] = dot(
                nrm[...], wq2[:, (j + 1) * 512 : (j + 2) * 512]
            ).astype(BF16)
        qs[...] = dot(nrm[2 * R :, :], wq2[:, 0:512]).astype(BF16)
        pairs = [(t, hd) for t in range(2) for hd in range(HEADS)]
        scores = []
        for t, hd in pairs:
            q = qs[t * R : (t + 1) * R, hd * HD : (hd + 1) * HD]
            k = kv[t * R : (t + 3) * R, hd * HD : (hd + 1) * HD]
            scores.append(
                lax.dot_general(q, k, (((1,), (1,)), ((), ())), preferred_element_type=F32)
            )
        allowed = []
        for t in range(2):
            ok1 = jnp.where((col * 2 + t) >= 1, pats[t, 0:1, 0 : 3 * R], 0.0) > 0.5
            ok2 = jnp.where((col * 2 + t) >= 2, pats[t, 4:5, 0 : 3 * R], 0.0) > 0.5
            allowed.append(causal | (back1 & ok1) | (back2 & ok2))
        scores = [
            jnp.where(allowed[t], s * HD**-0.5, -1e30) for (t, _), s in zip(pairs, scores)
        ]
        tops = [jnp.max(s, axis=-1, keepdims=True) for s in scores]
        weights = [jnp.exp(s - top) for s, top in zip(scores, tops)]
        got = [
            dot(e.astype(BF16), kv[t * R : (t + 3) * R, 512 + hd * HD : 512 + (hd + 1) * HD])
            for (t, hd), e in zip(pairs, weights)
        ]
        totals = [jnp.sum(e, axis=-1, keepdims=True) for e in weights]
        for (t, hd), part, total in zip(pairs, got, totals):
            ctx[t * R : (t + 1) * R, hd * HD : (hd + 1) * HD] = (part / total).astype(BF16)
        both = dot(ctx[...], wa2[...])
        for t in range(2):
            block = st[2 + t, :, pl.ds(z0, ZC), :].reshape(R, 512).astype(F32)
            wide = block + both[t * R : (t + 1) * R, :]
            aa[t] = wide
            mi = rms(wide, g_mix[...]).astype(BF16)
            for j in range(4):
                mixin[t, :, j, pl.ds(z0, ZC), :] = mi[:, j * 128 : (j + 1) * 128].reshape(
                    4, ZC, 128
                )
        @pl.when(g >= HELD)
        def _():
            send_chunk(g)

        after[:, pl.ds(z0, ZC), :] = aa[h].reshape(4, ZC, 512)
        xm[zone, pl.ds(z0, ZC), :] = mixin[h, zone // 4, lax.rem(zone, 4), pl.ds(z0, ZC), :]
        return carry

    lax.fori_loop(0, NG, step, 0)

    locals_[1].wait()
    for slot in range(len(SLOTS)):
        remote(mixin.at[0, 0, 0], xm.at[zone], fw_s.at[slot], fw_r.at[slot], other).wait()

    def mixed(b):
        total = jnp.zeros((128, 128), F32)
        for k in range(3):
            weight = mx[b, k]
            live = jnp.where(k < degree[b], weight, jnp.zeros_like(weight))
            total += dot(live, xm[neighbours[k, b]])
        return total.astype(BF16)

    def block_of(o):
        return lax.rem(o // 8 + 1 + zone // 8, 2) * 8 + lax.rem(zone + o, 8)

    def back(o):
        b = block_of(o)
        return remote(stage.at[b], spat.at[zone], rt_s.at[o], rt_r.at[o], (tm, b))

    def send_back(o, carry):
        b = block_of(o)
        stage[b] = mixed(b)
        back(o).start()
        return carry

    lax.fori_loop(0, 8, send_back, 0)
    lax.fori_loop(9, 16, send_back, 0)
    spat[zone] = mixed(zone)

    for k in range(15):
        ag2(1, own_i, k).wait_recv()
        ag2(2, own_o, k).wait_recv()
    ag3(2, wi).start()
    ag3(3, wo).start()

    send_pat.wait_send()
    for g in range(NG):
        swap(g).wait_send()
        onward(g).wait_send()
        relay(g).wait_send()
    for k in range(7):
        ag1(0, src_kv, own_kv, k).wait_send()
        ag1(1, src_i, own_i, k).wait_send()
        ag1(2, src_o, own_o, k).wait_send()
        ag1(3, src_q, own_q, k).wait_send()
    for k in range(15):
        ag2(0, own_kv, k).wait_send()
        ag2(1, own_i, k).wait_send()
        ag2(2, own_o, k).wait_send()
        ag2(3, own_q, k).wait_send()
    ag3(0, wq).wait_send()
    ag3(1, wa).wait_send()
    ag3(2, wi).wait()
    ag3(3, wo).wait()

    wi2, wo2 = wi.reshape(512, 2048), wo.reshape(2048, 512)
    written = []
    for turn in range(2):
        half = lax.rem(zone // 8 + turn, 2)
        for o in range(0, 8) if turn else range(9, 16):
            back(o).wait()
        for i in range(2):
            t = half * 2 + i
            wide = after[t] + jnp.concatenate(
                [spat[t * 4 + j].astype(F32) for j in range(4)], axis=1
            )
            acc[i * 128 : (i + 1) * 128, :] = wide
            nf[i * 128 : (i + 1) * 128, :] = rms(wide, g_ffn[...]).astype(BF16)
        for j in range(4):
            hidden = jax.nn.gelu(
                dot(nf[...], wi2[:, j * 512 : (j + 1) * 512]), approximate=True
            ).astype(BF16)
            acc[...] += dot(hidden, wo2[j * 512 : (j + 1) * 512, :])
        result[turn] = acc[...].astype(BF16).reshape(2, 128, 512)
        written.append(
            pltpu.make_async_copy(
                result.at[turn], out.at[pl.ds(half * 2, 2)], loc_sem.at[turn]
            )
        )
        written[turn].start()
    for cp in written:
        cp.wait()


def on_device(
    states, gain_attn, w_qkv, w_out_attn, pattern, gain_mix, neighbours, degree, mix, gain_ffn,
    w_in, w_out,
):
    hbm = pl.BlockSpec(memory_space=pl.ANY)
    dma = pltpu.SemaphoreType.DMA
    return pl.pallas_call(
        kernel,
        out_shape=jax.ShapeDtypeStruct(states.shape, BF16),
        in_specs=[hbm] * 12,
        out_specs=hbm,
        scratch_shapes=[
            pltpu.VMEM((8, 256), F32),
            pltpu.VMEM((1, 512), F32),
            pltpu.VMEM((1, 512), F32),
            pltpu.VMEM((1, 512), F32),
            pltpu.SMEM((1, 2), jnp.int32),
            pltpu.SMEM((3, 16), jnp.int32),
            pltpu.SMEM((16,), jnp.int32),
            pltpu.VMEM((4, 4, 128, 512), BF16),
            pltpu.VMEM((8, 2, 2, 16, 1536), BF16),
            pltpu.VMEM((8, 2, 2, 16, 512), BF16),
            pltpu.VMEM((8, 2, 2, 16, 2048), BF16),
            pltpu.VMEM((8, 2, 8, 16, 512), BF16),
            pltpu.VMEM((16, 3, 128, 128), BF16),
            pltpu.VMEM((2, 8, 256), F32),
            pltpu.VMEM((4 * R, 512), BF16),
            pltpu.VMEM((4 * R, 1024), BF16),
            pltpu.VMEM((2 * R, 512), BF16),
            pltpu.VMEM((2 * R, 512), BF16),
            pltpu.VMEM((2, R, 512), F32),
            pltpu.VMEM((4, 128, 512), F32),
            pltpu.VMEM((2, 4, 4, 128, 128), BF16),
            pltpu.VMEM((16, 128, 128), BF16),
            pltpu.VMEM((16, 128, 128), BF16),
            pltpu.VMEM((16, 128, 128), BF16),
            pltpu.VMEM((256, 512), BF16),
            pltpu.VMEM((256, 512), F32),
            pltpu.VMEM((2, 2, 128, 512), BF16),
            dma((12,)),
            dma((4, 7)), dma((4, 7)),
            dma((4, 15)), dma((4, 15)),
            dma((4,)), dma((4,)),
            dma((NG,)), dma((NG,)),
            dma, dma,
            dma((2, NG)), dma((2, NG)),
            dma((len(SLOTS),)), dma((len(SLOTS),)),
            dma((16,)), dma((16,)),
        ],
        compiler_params=pltpu.CompilerParams(
            collective_id=0, has_side_effects=True, vmem_limit_bytes=60 << 20
        ),
        cost_estimate=pl.CostEstimate(
            flops=5 * 10**9, bytes_accessed=8 * 10**6, transcendentals=2 * 10**6
        ),
        name="layer",
    )(
        states, w_qkv, w_out_attn, w_in, w_out, mix,
        gain_attn.reshape(1, -1), gain_mix.reshape(1, -1), gain_ffn.reshape(1, -1),
        pattern, neighbours.T, degree,
    )


def solution(mesh):
    return jax.shard_map(
        on_device,
        mesh=mesh,
        in_specs=(
            P("tm", "zone", None),
            P(),
            P("zone", None),
            P("zone", None),
            P("tm", None),
            P(),
            P(),
            P(),
            P(),
            P(),
            P("zone", None),
            P("zone", None),
        ),
        out_specs=P("tm", "zone", None),
        check_vma=False,
    )
```
